32 devices in a mesh: seq: 8 (over y, x, core), mp: 4 (over z).
Axes of the slice: x: 2, y: 2, z: 4, core: 2. Of those that a mesh axis runs over, the one named last changes fastest.
Arguments:
- hidden_in: bfloat16 [4096, 5376], P('seq'), may hold values from -6 to 6
- norm_gain: float32 [5376], replicated, may hold values from 0.5 to 1.5
- query_weight: bfloat16 [5376, 512], P(None, 'mp'), as said below
- kv_weight: bfloat16 [5376, 1024], P(None, 'mp'), as said below
- out_weight: bfloat16 [512, 5376], P('mp'), may hold values from -0.75 to 0.75
Outputs:
- attn_out: bfloat16 [5376, 4096], P('mp', 'seq')
The draws below stay inside these ranges and needn't reach their ends.
Inputs may be any that keep to these rules, and one draw needn't show every extreme that they name: `query_weight`: query projection columns of mean zero scaled by the fan-in. `kv_weight`: key and value projection columns of mean zero; the columns of query heads 2j and 2j+1 are equal, one key-value head shared by the pair.
All inputs are finite; a program needn't handle non-finite values.
Results may differ from the reference program's by a relative error of at most 0.023.
Values may be sent and summed in bfloat16 or wider, within the bound.
No kernel may reach another device: no remote copies, remote signals or barrier semaphores. Data moves between devices by JAX's collectives and lax.ppermute only.
A program may use at most 64 MiB of HBM per device.

```python
import math
import jax
import jax.numpy as jnp
from jax import lax

D = 5376
HD = 128
WINDOW = 1024
HQ = 4
KVH = 2
TOKENS = 4096


def paired_weights(key):
    scale_in = 1.0 / math.sqrt(D)
    query_part = jax.random.normal(jax.random.fold_in(key, 11), (D, HQ, HD), jnp.float32) * scale_in
    key_noise = jax.random.normal(jax.random.fold_in(key, 12), (D, KVH, HD), jnp.float32) * scale_in
    value_part = jax.random.normal(jax.random.fold_in(key, 13), (D, KVH, HD), jnp.float32) * scale_in
    key_part = key_noise
    stacked = jnp.stack([key_part, value_part], axis=2)
    doubled = jnp.repeat(stacked, 2, axis=1).reshape(D, HQ * 2 * HD)
    return (query_part.reshape(D, HQ * HD), doubled)


def draw_query_weight(key, part):
    return paired_weights(key)[0].astype(jnp.bfloat16)


def draw_kv_weight(key, part):
    return paired_weights(key)[1].astype(jnp.bfloat16)


def spiked(entries, rng, source, target, parts, factor):
    owner, partner = [(jnp.arange(entries.shape[dim]) // (entries.shape[dim] // parts)).reshape([-1 if axis == dim else 1 for axis in range(entries.ndim)]) for dim in (source, target)]
    chosen = jax.random.permutation(rng, parts)[partner]
    strong = (owner == chosen) | (owner == (partner + parts // 2) % parts)
    return jnp.where(strong, factor * entries, entries)


def block_levels(rng, dims, split, low, top_value):
    loudness, own = 1.0, jax.random.fold_in(rng, 6)
    for dim, parts in split:
        steps = jnp.exp(jax.random.uniform(jax.random.fold_in(own, dim), (parts,), jnp.float32, low / len(split), top_value / len(split)))
        loudness = loudness * jnp.repeat(steps, dims[dim] // parts).reshape([-1 if axis == dim else 1 for axis in range(len(dims))])
    return loudness


def bell_draw(stream_key, extent, spread, reach, shards=(), held_as=jnp.bfloat16):
    factor_of = block_levels(stream_key, extent, shards, -0.22, 0.18) if shards else 1.0
    values = jax.random.normal(stream_key, extent, jnp.float32) * spread * factor_of
    return jnp.minimum(jnp.maximum(values, -reach), reach).astype(held_as)


def noise_with(stream_key, extent, spread, bound, split, heavy, kind=jnp.bfloat16):
    array = spread * jax.random.normal(stream_key, extent, jnp.float32)
    if split:
        array = array * block_levels(stream_key, extent, split, -0.22, 0.18)
    return jnp.clip(spiked(array, jax.random.fold_in(stream_key, 3), *heavy), -bound, bound).astype(kind)


def setup_inputs(seed: int = 0) -> dict:
    key_list = jax.random.split(jax.random.key(seed), 6)
    return {
        "hidden_in": bell_draw(key_list[0], (TOKENS, D), 1.0, 6.0, ((0, 8),)),
        "norm_gain": jnp.clip(jax.random.uniform(key_list[1], (D,), jnp.float32, 0.5, 1.5), 0.5, 1.5),
        "query_weight": draw_query_weight(jax.random.fold_in(key_list[5], 71), 0),
        "kv_weight": draw_kv_weight(jax.random.fold_in(key_list[5], 71), 0),
        "out_weight": noise_with(key_list[4], (HQ * HD, D), HD ** -0.5, 0.75, ((0, 4),), (0, 1, 4, 2.0)),
    }


def rotate_half(tensor, positions):
    half = tensor.shape[-1] // 2
    freq = jnp.exp(-math.log(10000.0) * jnp.arange(half, dtype=jnp.float32) * (2.0 / tensor.shape[-1]))
    angle = positions[:, None, None] * freq[None, None, :]
    cosine = jnp.cos(angle)
    sine = jnp.sin(angle)
    first = tensor[..., :half]
    second = tensor[..., half:]
    return jnp.concatenate([first * cosine - second * sine, second * cosine + first * sine], axis=-1)

def reference(hidden_in, norm_gain, query_weight, kv_weight, out_weight):
    length = hidden_in.shape[0]
    widths = hidden_in.astype(jnp.float32)
    inverse = lax.rsqrt(lax.optimization_barrier(jnp.mean(widths * widths, axis=-1, keepdims=True)) + 1e-06)
    normed = (widths * inverse * norm_gain.astype(jnp.float32)[None, :]).astype(jnp.bfloat16)
    positions = jnp.arange(length).astype(jnp.float32)
    queries = jnp.dot(normed, query_weight, preferred_element_type=jnp.float32).reshape(length, HQ, HD)
    queries = rotate_half(queries, positions).astype(jnp.bfloat16)
    projected = jnp.dot(normed, kv_weight, preferred_element_type=jnp.float32).reshape(length, HQ, 2, HD)
    keys = rotate_half(projected[:, :, 0, :], positions).astype(jnp.bfloat16)
    values = projected[:, :, 1, :].astype(jnp.bfloat16)
    block = math.gcd(length, 512)
    pad_keys = jnp.concatenate([jnp.zeros((WINDOW, HQ, HD), jnp.bfloat16), keys], axis=0)
    pad_values = jnp.concatenate([jnp.zeros((WINDOW, HQ, HD), jnp.bfloat16), values], axis=0)

    def one_block(index):
        offset = (index * block).astype(jnp.int32)
        query_block = lax.dynamic_slice_in_dim(queries, offset, block, 0)
        key_block = lax.dynamic_slice_in_dim(pad_keys, offset, WINDOW + block, 0)
        value_block = lax.dynamic_slice_in_dim(pad_values, offset, WINDOW + block, 0)
        scores = jnp.einsum('qhd,khd->hqk', query_block.astype(jnp.float32), key_block.astype(jnp.float32))
        scores = scores * (1.0 / math.sqrt(168.0))
        query_pos = offset + jnp.arange(block, dtype=jnp.int32)
        key_pos = offset - WINDOW + jnp.arange(WINDOW + block, dtype=jnp.int32)
        valid = (key_pos[None, :] <= query_pos[:, None]) & (query_pos[:, None] - key_pos[None, :] < WINDOW) & (key_pos[None, :] >= 0)
        scores = jnp.where(valid[None], scores, jnp.float32(-1e+30))
        highest = lax.optimization_barrier(jnp.max(scores, axis=-1, keepdims=True))
        expo = jnp.exp(scores - highest)
        probs = (expo / lax.optimization_barrier(jnp.sum(expo, axis=-1, keepdims=True))).astype(jnp.bfloat16)
        mixed = jnp.einsum('hqk,khd->qhd', probs.astype(jnp.float32), value_block.astype(jnp.float32))
        return mixed.astype(jnp.bfloat16).reshape(block, HQ * HD)
    head_out = lax.map(one_block, jnp.arange(length // block, dtype=jnp.int32)).reshape(length, HQ * HD)

    def add_head(total, head):
        start_col = (head * HD).astype(jnp.int32)
        part_out = lax.dynamic_slice_in_dim(head_out, start_col, HD, 1)
        part_weight = lax.dynamic_slice_in_dim(out_weight, start_col, HD, 0)
        term = jnp.dot(part_out, part_weight, preferred_element_type=jnp.float32).astype(jnp.bfloat16)
        term = lax.optimization_barrier(term)
        return (total + term.astype(jnp.float32), None)
    summed, unused = lax.scan(add_head, jnp.zeros((length, D), jnp.float32), jnp.arange(HQ, dtype=jnp.int32))
    return summed.T.astype(jnp.bfloat16)
```

```python
import functools
import math

import jax
import jax.numpy as jnp
import numpy as np
from jax import lax
from jax.experimental import pallas as pl
from jax.experimental.pallas import tpu as pltpu
from jax.sharding import PartitionSpec as P

WINDOW = 1024
LANES = 128
MASKED = -1e30
F32 = jnp.float32
BF16 = jnp.bfloat16


def around(block, axis, distance):
    size = lax.axis_size(axis)
    return lax.ppermute(block, axis, [(i, (i + distance) % size) for i in range(size)])


def other_core(block):
    return lax.ppermute(block, "seq", [(i, i ^ 1) for i in range(lax.axis_size("seq"))])


def call(kernel, name, out_shape, cost, vmem=48 * 2**20, **kwargs):
    flops, moved = cost
    return pl.pallas_call(
        kernel,
        name=name,
        out_shape=out_shape,
        cost_estimate=pl.CostEstimate(flops=flops, bytes_accessed=moved, transcendentals=0),
        compiler_params=pltpu.CompilerParams(vmem_limit_bytes=vmem),
        **kwargs,
    )


def matmul(left, right, dims=((1,), (0,))):
    return lax.dot_general(left, right, (dims, ((), ())), preferred_element_type=F32)


def rope_table(rows, head):
    freq = np.exp(-math.log(10000.0) * np.arange(head // 2) * (2.0 / head))
    angle = np.arange(rows)[:, None] * freq[None, :]
    return np.concatenate([np.cos(angle), np.sin(angle)], axis=1).astype(np.float32)


def rope(tensor, table, first_pos):
    head = tensor.shape[1]
    half = head // 2
    lane = lax.broadcasted_iota(jnp.int32, (1, head), 1)
    low = lane < half
    index = jnp.where(low, lane, lane - half).astype(F32)
    base = first_pos * jnp.exp(index * (-math.log(10000.0) * 2.0 / head))
    base_cos = jnp.cos(base)
    base_sin = jnp.where(low, -jnp.sin(base), jnp.sin(base))
    turned = pltpu.roll(table, half, 1)
    row_cos = jnp.where(low, table, turned)
    row_sin = jnp.where(low, -turned, table)
    cosine = base_cos * row_cos - base_sin * row_sin
    sine = base_sin * row_cos + base_cos * row_sin
    return tensor * cosine + pltpu.roll(tensor, half, 1) * sine


def project_kernel(finish, steps, width, x_ref, gain_ref, weight_ref, table_ref, *refs):
    outs, (total_ref, square_ref) = refs[:-2], refs[-2:]
    step = pl.program_id(0)

    @pl.when(step == 0)
    def _():
        total_ref[...] = jnp.zeros_like(total_ref)
        square_ref[...] = jnp.zeros_like(square_ref)

    x = x_ref[...].astype(F32)
    squares = x * x
    part = squares[:, :LANES]
    for start in range(LANES, x.shape[1], LANES):
        part = part + squares[:, start : start + LANES]
    square_ref[...] += part
    scaled = (x * gain_ref[...]).astype(BF16)
    total_ref[...] += matmul(scaled, weight_ref[...])

    @pl.when(step == steps - 1)
    def _():
        mean = jnp.sum(square_ref[...], axis=1, keepdims=True) * (1.0 / width)
        result = total_ref[...] * lax.rsqrt(mean + 1e-06)
        finish(result, table_ref[...], *outs)


def finish_keys_values(head, result, table, key_ref, value_ref):
    rows = result.shape[0]
    first_pos = (lax.axis_index("seq") * rows).astype(F32)
    key_ref[...] = rope(result[:, :head], table, first_pos).astype(BF16)
    value_ref[...] = result[:, head:].T.astype(BF16)


def finish_queries(scale, result, table, query_ref):
    rows = result.shape[0]
    first_pos = (lax.axis_index("seq") * rows).astype(F32)
    query_ref[...] = (rope(result, table, first_pos) * scale).astype(BF16)


def project(finish, name, hidden, gain, weight, table, out_shapes):
    rows, width = hidden.shape
    cols = weight.shape[1]
    block = 768 if width % 768 == 0 else width
    steps = width // block
    whole = lambda shape: pl.BlockSpec(shape, lambda k: (0, 0))
    return call(
        functools.partial(project_kernel, finish, steps, width),
        name,
        out_shapes,
        (2 * rows * width * cols, 2 * width * (rows + cols)),
        grid=(steps,),
        in_specs=[
            pl.BlockSpec((rows, block), lambda k: (0, k)),
            pl.BlockSpec((1, block), lambda k: (0, k)),
            pl.BlockSpec((block, cols), lambda k: (k, 0)),
            whole(table.shape),
        ],
        out_specs=[whole(s.shape) for s in out_shapes],
        scratch_shapes=[pltpu.VMEM((rows, cols), F32), pltpu.VMEM((rows, LANES), F32)],
    )(hidden, gain, weight, table)


def attention_kernel(q_ref, k0_ref, k1_ref, k2_ref, v0_ref, v1_ref, v2_ref, out_ref):
    rows = q_ref.shape[0]
    chunk = min(rows, 256)
    shard = lax.axis_index("seq")
    bias1 = jnp.where(shard < 1, MASKED, 0.0).astype(F32)
    bias2 = jnp.where(shard < 2, MASKED, 0.0).astype(F32)
    nt = ((1,), (1,))
    for start in range(0, rows, chunk):
        q = q_ref[start : start + chunk, :]
        key_index = lax.broadcasted_iota(jnp.int32, (rows, chunk), 0)
        query_index = lax.broadcasted_iota(jnp.int32, (rows, chunk), 1) + start
        own = key_index <= query_index
        near = matmul(k1_ref[...], q, nt) + bias1
        mixed = jnp.where(own, matmul(k0_ref[...], q, nt), matmul(k2_ref[...], q, nt) + bias2)
        highest = jnp.maximum(
            jnp.max(near, axis=0, keepdims=True), jnp.max(mixed, axis=0, keepdims=True)
        )
        near = jnp.exp2(near - highest)
        mixed = jnp.exp2(mixed - highest)
        norm = jnp.sum(near, axis=0, keepdims=True) + jnp.sum(mixed, axis=0, keepdims=True)
        out = matmul(v1_ref[...], near.astype(BF16))
        out += matmul(v0_ref[...], jnp.where(own, mixed, 0.0).astype(BF16))
        out += matmul(v2_ref[...], jnp.where(own, 0.0, mixed).astype(BF16))
        out_ref[:, start : start + chunk] = (out / norm).astype(BF16)


def attention(q, keys, values):
    rows, head = q.shape
    return call(
        attention_kernel,
        "attention",
        jax.ShapeDtypeStruct((head, rows), BF16),
        (12 * rows * rows * head, 16 * rows * head),
    )(q, *keys, *values)


def weight_window(width, mp):
    cols = width // mp
    tiles = max(-(-cols * (m + 1) // LANES) - cols * m // LANES for m in range(mp))
    return cols, tiles


def window_start(m, width, mp):
    cols, tiles = weight_window(width, mp)
    first = jnp.minimum(m * cols // LANES, width // LANES - tiles)
    return pl.multiple_of(first * LANES, LANES)


def cut_kernel(width, mp, weight_ref, *refs):
    outs, sems = refs[:-1], refs[-1]
    half, window = outs[0].shape
    m = lax.axis_index("mp")
    core = lax.axis_index("seq") % 2
    row = pl.multiple_of(core * half, half)
    copies = []
    for distance, out in enumerate(outs, 1):
        start = window_start((m + distance) % mp, width, mp)
        copies.append(
            pltpu.make_async_copy(
                weight_ref.at[pl.ds(row, half), pl.ds(start, window)], out, sems.at[distance - 1]
            )
        )
    for copy in copies:
        copy.start()
    for copy in copies:
        copy.wait()


def turn_kernel(width, mp, weight_ref, *refs):
    mine, theirs = refs[: mp - 1], refs[mp - 1 : 2 * mp - 2]
    out_ref, own_ref, sem = refs[2 * mp - 2 :]
    head, window = own_ref.shape
    half = head // 2
    m = lax.axis_index("mp")
    core = lax.axis_index("seq") % 2
    start = window_start(m, width, mp)
    copy = pltpu.make_async_copy(weight_ref.at[:, pl.ds(start, window)], own_ref, sem)
    copy.start()
    for i in range(mp - 1):
        a, b = mine[i][...], theirs[i][...]
        low = jnp.where(core == 0, a, b)
        high = jnp.where(core == 0, b, a)
        both = jnp.concatenate([low, high], axis=0)
        out_ref[:, (i + 1) * head : (i + 2) * head] = both.T
    copy.wait()
    out_ref[:, :head] = own_ref[...].T


def output_kernel(width, mp, chunk, weight_ref, *refs):
    heads, out_ref = refs[:-1], refs[-1]
    m = lax.axis_index("mp")
    cols = width // mp
    offset = m * cols - window_start(m, width, mp) + pl.program_id(0) * chunk
    weight = weight_ref[pl.ds(pl.multiple_of(offset, 16), chunk), :]
    taken = jnp.concatenate([h[...] for h in heads], axis=0)
    out_ref[...] = matmul(weight, taken).astype(BF16)


def per_device(hidden_in, norm_gain, query_weight, kv_weight, out_weight):
    rows, width = hidden_in.shape
    head = query_weight.shape[1]
    mp = lax.axis_size("mp")
    cols, tiles = weight_window(width, mp)
    window = tiles * LANES
    half = head // 2
    gain = norm_gain[None, :]
    table = jnp.asarray(rope_table(rows, head))
    anywhere = pl.BlockSpec(memory_space=pl.ANY)
    shape = lambda *dims: jax.ShapeDtypeStruct(dims, BF16)

    pieces = call(
        functools.partial(cut_kernel, width, mp),
        "cut_weight",
        [shape(half, window)] * (mp - 1),
        (0, 4 * (mp - 1) * half * window),
        in_specs=[anywhere],
        out_specs=[anywhere] * (mp - 1),
        scratch_shapes=[pltpu.SemaphoreType.DMA((mp - 1,))],
    )(out_weight)
    mine = [around(piece, "mp", d) for d, piece in enumerate(pieces, 1)]

    keys, values = project(
        functools.partial(finish_keys_values, head),
        "keys_values",
        hidden_in,
        gain,
        kv_weight,
        table,
        [shape(rows, head), shape(head, rows)],
    )
    key_parts = [keys] + [around(keys, "seq", d) for d in (1, 2)]
    value_parts = [values] + [around(values, "seq", d) for d in (1, 2)]
    scale = math.log2(math.e) / math.sqrt(168.0)
    (queries,) = project(
        functools.partial(finish_queries, scale),
        "queries",
        hidden_in,
        gain,
        query_weight,
        table,
        [shape(rows, head)],
    )
    head_out = attention(queries, key_parts, value_parts)
    outs = [head_out] + [around(head_out, "mp", d) for d in range(1, mp)]

    theirs = [other_core(piece) for piece in mine]
    turned = call(
        functools.partial(turn_kernel, width, mp),
        "turn_weight",
        shape(window, mp * head),
        (0, 4 * window * mp * head),
        in_specs=[anywhere] + [pl.BlockSpec(memory_space=pltpu.VMEM)] * (2 * mp - 2),
        scratch_shapes=[pltpu.VMEM((head, window), BF16), pltpu.SemaphoreType.DMA],
    )(out_weight, *mine, *theirs)

    chunk = max(c for c in range(16, min(cols, 448) + 1, 16) if cols % c == 0)
    return call(
        functools.partial(output_kernel, width, mp, chunk),
        "output",
        shape(cols, rows),
        (2 * cols * rows * mp * head, 2 * cols * (rows + mp * head)),
        grid=(cols // chunk,),
        in_specs=[pl.BlockSpec(memory_space=pltpu.VMEM)] * (mp + 1),
        out_specs=pl.BlockSpec((chunk, rows), lambda i: (i, 0)),
    )(turned, *outs)


def solution(mesh):
    in_specs = (P("seq", None), P(), P(None, "mp"), P(None, "mp"), P("mp", None))
    out_specs = P("mp", "seq")
    return jax.shard_map(
        per_device, mesh=mesh, in_specs=in_specs, out_specs=out_specs, check_vma=False
    )
```

```python
import functools
import math

import jax
import jax.numpy as jnp
import numpy as np
from jax import lax
from jax.experimental import pallas as pl
from jax.experimental.pallas import tpu as pltpu
from jax.sharding import PartitionSpec as P

WINDOW = 1024
LANES = 128
MASKED = -1e30
F32 = jnp.float32
BF16 = jnp.bfloat16


def around(block, axis, distance):
    size = lax.axis_size(axis)
    return lax.ppermute(block, axis, [(i, (i + distance) % size) for i in range(size)])


def other_core(block):
    return lax.ppermute(block, "seq", [(i, i ^ 1) for i in range(lax.axis_size("seq"))])


def call(kernel, name, out_shape, vmem=16 * 2**20, flops=1, **kwargs):
    return pl.pallas_call(
        kernel,
        name=name,
        out_shape=out_shape,
        cost_estimate=pl.CostEstimate(flops=flops, bytes_accessed=1, transcendentals=0),
        compiler_params=pltpu.CompilerParams(vmem_limit_bytes=vmem),
        **kwargs,
    )


def matmul(left, right, dims=((1,), (0,))):
    return lax.dot_general(left, right, (dims, ((), ())), preferred_element_type=F32)


def rope_factors(rope_ref, first_pos):
    rows, head = rope_ref.shape[1:]
    half = head // 2
    step = 8

    def turn(count, stride, start):
        lane = lax.broadcasted_iota(jnp.int32, (count, head), 1)
        low = lane < half
        freq = jnp.exp(
            jnp.where(low, lane, lane - half).astype(F32) * (-math.log(10000.0) * 2.0 / head)
        )
        place = lax.broadcasted_iota(jnp.int32, (count, head), 0) * stride + start
        angle = place.astype(F32) * freq
        return jnp.cos(angle), jnp.sin(angle), jnp.where(low, -1.0, 1.0)

    fine_cos, fine_sin, _ = turn(step, 1, 0)
    coarse_cos, coarse_sin, sign = turn(rows // step, step, first_pos)
    for a in range(rows // step):
        span = slice(a * step, (a + 1) * step)
        c, s = coarse_cos[a : a + 1, :], coarse_sin[a : a + 1, :]
        rope_ref[0, span, :] = c * fine_cos - s * fine_sin
        rope_ref[1, span, :] = (s * fine_cos + c * fine_sin) * sign[:step, :]


def rope(tensor, cosine, sine):
    return tensor * cosine + pltpu.roll(tensor, tensor.shape[1] // 2, 1) * sine


def project_kernel(finish, block, ahead, x_ref, gain_ref, weight_ref, out_ref, *scratch):
    x_buf, gain_buf, weight_buf, rope_buf, scaled_ref, total_ref, square_ref, sems = scratch
    rows, width = x_ref.shape
    steps = width // block
    gain_copy = pltpu.make_async_copy(gain_ref, gain_buf, sems.at[2, 0])
    copies = []
    for k in range(steps):
        part = pl.ds(k * block, block)
        copies.append(
            (
                pltpu.make_async_copy(x_ref.at[:, part], x_buf.at[:, part], sems.at[0, k]),
                pltpu.make_async_copy(
                    weight_ref.at[part, :], weight_buf.at[part, :], sems.at[1, k]
                ),
            )
        )
    gain_copy.start()
    for pair in copies[:ahead]:
        for copy in pair:
            copy.start()
    rope_factors(rope_buf, lax.axis_index("seq") * rows)
    gain_copy.wait()
    chunk = 64
    for k in range(steps):
        for copy in copies[k]:
            copy.wait()
        if k + ahead < steps:
            for copy in copies[k + ahead]:
                copy.start()
        for r in range(0, rows, chunk):
            part = None
            for t in range(k * block, (k + 1) * block, LANES):
                x = x_buf[r : r + chunk, t : t + LANES]
                gain = gain_buf[t // LANES : t // LANES + 1, :].astype(BF16)
                scaled_ref[r : r + chunk, t : t + LANES] = x * gain
                square = x * x
                part = square if part is None else part + square
            part = part.astype(F32)
            square_ref[r : r + chunk, :] = part if k == 0 else square_ref[r : r + chunk, :] + part
        span = slice(k * block, (k + 1) * block)
        product = matmul(scaled_ref[:, span], weight_buf[span, :])
        total_ref[...] = product if k == 0 else total_ref[...] + product
    mean = jnp.sum(square_ref[...], axis=1, keepdims=True) * (1.0 / width)
    finish(total_ref, lax.rsqrt(mean + 1e-06), rope_buf, out_ref)


def keys_values_kernel(width, mp, block, ahead, cut, x_ref, gain_ref, weight_ref, *refs):
    out_weight_ref, first_piece_ref, kv_ref, *refs = refs
    pieces, scratch, cut_sems = refs[: len(cut)], refs[len(cut) : -1], refs[-1]
    copies = cut_copies(width, mp, cut, out_weight_ref, pieces, cut_sems)
    finish = functools.partial(finish_keys_values, copies)
    project_kernel(finish, block, ahead, x_ref, gain_ref, weight_ref, kv_ref, *scratch)
    for copy in copies:
        copy.wait()


def finish_keys_values(copies, total_ref, inverse, rope_buf, out_ref):
    for copy in copies:
        copy.start()
    rows = total_ref.shape[0]
    head = total_ref.shape[1] // 2
    keys = total_ref[:, :head] * inverse
    out_ref[:rows, :] = rope(keys, rope_buf[0], rope_buf[1]).astype(BF16)
    for t in range(rows // LANES):
        span = slice(t * LANES, (t + 1) * LANES)
        values = total_ref[span, head:] * inverse[span, :]
        out_ref[rows + t * head : rows + (t + 1) * head, :] = values.T.astype(BF16)


def finish_queries(scale, total_ref, inverse, rope_buf, out_ref):
    queries = rope(total_ref[...] * inverse, rope_buf[0], rope_buf[1])
    out_ref[...] = (queries * scale).astype(BF16)


def queries_kernel(scale, block, ahead, x_ref, gain_ref, weight_ref, first_piece_ref, *refs):
    finish = functools.partial(finish_queries, scale)
    project_kernel(finish, block, ahead, x_ref, gain_ref, weight_ref, *refs)


BLOCK = 768
AHEAD = 4


def project_scratch(rows, width, cols, head):
    return [
        pltpu.VMEM((rows, width), BF16),
        pltpu.VMEM((width // LANES, LANES), F32),
        pltpu.VMEM((width, cols), BF16),
        pltpu.VMEM((2, rows, head), F32),
        pltpu.VMEM((rows, width), BF16),
        pltpu.VMEM((rows, cols), F32),
        pltpu.VMEM((rows, LANES), F32),
        pltpu.SemaphoreType.DMA((3, max(2, width // BLOCK))),
    ]


def values_of(block_ref, rows):
    head = block_ref.shape[1]
    tiles = [block_ref[rows + t * head : rows + (t + 1) * head, :] for t in range(rows // LANES)]
    return jnp.concatenate(tiles, axis=1)


def attention_kernel(q_ref, kv0_ref, kv1_ref, kv2_ref, out_ref):
    rows, head = q_ref.shape
    chunk = min(rows, 256)
    shard = lax.axis_index("seq")
    bias1 = jnp.where(shard < 1, MASKED, 0.0).astype(F32)
    bias2 = jnp.where(shard < 2, MASKED, 0.0).astype(F32)
    nt = ((1,), (1,))
    values = [values_of(ref, rows) for ref in (kv0_ref, kv1_ref, kv2_ref)]
    for start in range(0, rows, chunk):
        span = slice(start, start + chunk)
        q = q_ref[span, :]
        key_index = lax.broadcasted_iota(jnp.int32, (rows, chunk), 0)
        query_index = lax.broadcasted_iota(jnp.int32, (rows, chunk), 1) + start
        own = key_index <= query_index
        near = matmul(kv1_ref[:rows, :], q, nt) + bias1
        far = matmul(kv2_ref[:rows, :], q, nt) + bias2
        mixed = jnp.where(own, matmul(kv0_ref[:rows, :], q, nt), far)
        highest = jnp.maximum(
            jnp.max(near, axis=0, keepdims=True), jnp.max(mixed, axis=0, keepdims=True)
        )
        near = jnp.exp2(near - highest)
        mixed = jnp.exp2(mixed - highest)
        norm = jnp.sum(near, axis=0, keepdims=True) + jnp.sum(mixed, axis=0, keepdims=True)
        out = matmul(values[1], near.astype(BF16))
        out += matmul(values[0], jnp.where(own, mixed, 0.0).astype(BF16))
        out += matmul(values[2], jnp.where(own, 0.0, mixed).astype(BF16))
        out_ref[:, span] = (out * (1.0 / norm)).astype(BF16)


def weight_window(width, mp):
    cols = width // mp
    tiles = max(-(-cols * (m + 1) // LANES) - cols * m // LANES for m in range(mp))
    return cols, tiles


def window_start(m, width, mp):
    cols, tiles = weight_window(width, mp)
    first = jnp.minimum(m * cols // LANES, width // LANES - tiles)
    return pl.multiple_of(first * LANES, LANES)


def cut_copies(width, mp, distances, weight_ref, outs, sems):
    m = lax.axis_index("mp")
    core = lax.axis_index("seq") % 2
    copies = []
    for i, (distance, out) in enumerate(zip(distances, outs)):
        half, window = out.shape
        row = pl.multiple_of(core * half, half)
        start = window_start((m + distance) % mp, width, mp)
        source = weight_ref.at[pl.ds(row, half), pl.ds(start, window)]
        copies.append(pltpu.make_async_copy(source, out, sems.at[i]))
    return copies


def cut_kernel(width, mp, distances, weight_ref, *refs):
    copies = cut_copies(width, mp, distances, weight_ref, refs[:-1], refs[-1])
    for copy in copies:
        copy.start()
    for copy in copies:
        copy.wait()


def turn_kernel(width, mp, weight_ref, *refs):
    pieces, (out_ref, own_ref, sem) = refs[: mp - 1], refs[-3:]
    half, window = own_ref.shape
    (copy,) = cut_copies(width, mp, [0], weight_ref, [own_ref], sem)
    copy.start()
    pair = []
    copy.wait()
    for i, piece in enumerate([own_ref, *pieces]):
        pair.append(piece[...])
        if i % 2:
            out_ref[:, (i - 1) * half : (i + 1) * half] = jnp.concatenate(pair, axis=0).T
            pair = []


def collect_kernel(*refs):
    heads, out_ref = refs[:-1], refs[-1]
    head = heads[0].shape[0]
    half = head // 2
    core = lax.axis_index("seq") % 2
    for i, block in enumerate(heads):
        for place in range(2):
            row = pl.multiple_of((core if place == 0 else 1 - core) * half, half)
            to = (place * len(heads) + i) * half
            out_ref[to : to + half, :] = block[pl.ds(row, half), :]


def output_kernel(width, mp, chunk, mine_ref, theirs_ref, heads_ref, out_ref, buf_ref, sems):
    cols = out_ref.shape[0]
    m = lax.axis_index("mp")
    offset = m * cols - window_start(m, width, mp)
    half = mine_ref.shape[1]
    copies = []
    for i in range(cols // chunk):
        span = pl.ds(i * chunk, chunk)
        rows = pl.ds(pl.multiple_of(offset + i * chunk, 16), chunk)
        total = matmul(mine_ref[rows, :], heads_ref[:half, :])
        total += matmul(theirs_ref[rows, :], heads_ref[half:, :])
        buf_ref[span, :] = total.astype(BF16)
        copies.append(pltpu.make_async_copy(buf_ref.at[span, :], out_ref.at[span, :], sems.at[i]))
        copies[-1].start()
    for copy in copies:
        copy.wait()


def per_device(hidden_in, norm_gain, query_weight, kv_weight, out_weight):
    rows, width = hidden_in.shape
    head = query_weight.shape[1]
    mp = lax.axis_size("mp")
    assert 2 * rows == WINDOW and width % BLOCK == 0 and head == LANES
    cols, tiles = weight_window(width, mp)
    window = tiles * LANES
    half = head // 2
    gain = norm_gain.reshape(width // LANES, LANES)
    hbm = pl.BlockSpec(memory_space=pltpu.HBM)
    vmem = pl.BlockSpec(memory_space=pltpu.VMEM)
    dma = pltpu.SemaphoreType.DMA
    shape = lambda *dims: jax.ShapeDtypeStruct(dims, BF16)
    large = 52 * 2**20

    order = sorted(range(1, mp), key=lambda d: abs(d - mp // 2))
    first, later = order[:1], order[1:]
    pieces = call(
        functools.partial(cut_kernel, width, mp, first),
        "cut_weight",
        [shape(half, window)] * len(first),
        vmem=large,
        in_specs=[hbm],
        out_specs=[vmem] * len(first),
        scratch_shapes=[dma((len(first),))],
    )(out_weight)
    kv, *rest = call(
        functools.partial(keys_values_kernel, width, mp, BLOCK, AHEAD, later),
        "keys_values",
        [shape(2 * rows, head)] + [shape(half, window)] * len(later),
        vmem=large,
        in_specs=[hbm] * 4 + [pl.BlockSpec(memory_space=pl.ANY)],
        out_specs=[vmem] * (1 + len(later)),
        scratch_shapes=project_scratch(rows, width, 2 * head, head) + [dma((len(later),))],
    )(hidden_in, gain, kv_weight, out_weight, pieces[0])
    kv2 = around(kv, "seq", 2)
    kv1 = around(kv, "seq", 1)
    mine = [around(piece, "mp", d) for d, piece in zip(order, list(pieces) + rest)]
    scale = math.log2(math.e) / math.sqrt(168.0)
    queries = call(
        functools.partial(queries_kernel, scale, BLOCK, AHEAD),
        "queries",
        shape(rows, head),
        vmem=large,
        flops=2 * 10**10,
        in_specs=[hbm] * 3 + [pl.BlockSpec(memory_space=pl.ANY)],
        out_specs=vmem,
        scratch_shapes=project_scratch(rows, width, head, head),
    )(hidden_in, gain, query_weight, mine[0])
    head_out = call(
        attention_kernel,
        "attention",
        shape(head, rows),
        in_specs=[vmem] * 4,
        out_specs=vmem,
    )(queries, kv, kv1, kv2)
    heads = [head_out] + [around(head_out, "mp", d) for d in order]

    mine_turned = call(
        functools.partial(turn_kernel, width, mp),
        "turn_weight",
        shape(window, mp * half),
        in_specs=[hbm] + [vmem] * (mp - 1) + [pl.BlockSpec(memory_space=pl.ANY)],
        out_specs=vmem,
        scratch_shapes=[pltpu.VMEM((half, window), BF16), dma((1,))],
    )(out_weight, *mine, head_out)
    theirs_turned = other_core(mine_turned)
    taken = call(
        collect_kernel,
        "collect_heads",
        shape(mp * head, rows),
        flops=3 * 10**10,
        in_specs=[vmem] * mp,
        out_specs=vmem,
    )(*heads)

    chunk = max(c for c in range(16, min(cols, 448) + 1, 16) if cols % c == 0)
    return call(
        functools.partial(output_kernel, width, mp, chunk),
        "output",
        shape(cols, rows),
        in_specs=[vmem] * 3,
        out_specs=hbm,
        scratch_shapes=[pltpu.VMEM((cols, rows), BF16), dma((cols // chunk,))],
    )(mine_turned, theirs_turned, taken)


def solution(mesh):
    in_specs = (P("seq", None), P(), P(None, "mp"), P(None, "mp"), P("mp", None))
    out_specs = P("mp", "seq")
    return jax.shard_map(
        per_device, mesh=mesh, in_specs=in_specs, out_specs=out_specs, check_vma=False
    )
```

```python
import functools
import math

import jax
import jax.numpy as jnp
import numpy as np
from jax import lax
from jax.experimental import pallas as pl
from jax.experimental.pallas import tpu as pltpu
from jax.sharding import PartitionSpec as P

WINDOW = 1024
LANES = 128
MASKED = -1e30
F32 = jnp.float32
BF16 = jnp.bfloat16


def around(block, axis, distance):
    size = lax.axis_size(axis)
    return lax.ppermute(block, axis, [(i, (i + distance) % size) for i in range(size)])


def other_core(block):
    return lax.ppermute(block, "seq", [(i, i ^ 1) for i in range(lax.axis_size("seq"))])


def next_chip(block):
    return lax.ppermute(block, "seq", [(i, i ^ 2) for i in range(lax.axis_size("seq"))])


def partner(m, distance, mp):
    return m ^ distance if mp == 4 else (m + distance) % mp


def exchanged(block, distance):
    mp = lax.axis_size("mp")
    return lax.ppermute(block, "mp", [(i, partner(i, distance, mp)) for i in range(mp)])


def call(kernel, name, out_shape, vmem=16 * 2**20, flops=1, **kwargs):
    return pl.pallas_call(
        kernel,
        name=name,
        out_shape=out_shape,
        cost_estimate=pl.CostEstimate(flops=flops, bytes_accessed=1, transcendentals=0),
        compiler_params=pltpu.CompilerParams(vmem_limit_bytes=vmem),
        **kwargs,
    )


def matmul(left, right, dims=((1,), (0,))):
    return lax.dot_general(left, right, (dims, ((), ())), preferred_element_type=F32)


def rope_factors(rope_ref, first_pos):
    rows, head = rope_ref.shape[1:]
    half = head // 2
    step = 8

    def turn(count, stride, start):
        lane = lax.broadcasted_iota(jnp.int32, (count, head), 1)
        low = lane < half
        freq = jnp.exp(
            jnp.where(low, lane, lane - half).astype(F32) * (-math.log(10000.0) * 2.0 / head)
        )
        place = lax.broadcasted_iota(jnp.int32, (count, head), 0) * stride + start
        angle = place.astype(F32) * freq
        return jnp.cos(angle), jnp.sin(angle), jnp.where(low, -1.0, 1.0)

    fine_cos, fine_sin, _ = turn(step, 1, 0)
    coarse_cos, coarse_sin, sign = turn(rows // step, step, first_pos)
    for a in range(rows // step):
        span = slice(a * step, (a + 1) * step)
        c, s = coarse_cos[a : a + 1, :], coarse_sin[a : a + 1, :]
        rope_ref[0, span, :] = c * fine_cos - s * fine_sin
        rope_ref[1, span, :] = (s * fine_cos + c * fine_sin) * sign[:step, :]


def rope(tensor, cosine, sine):
    return tensor * cosine + pltpu.roll(tensor, tensor.shape[1] // 2, 1) * sine


def project_kernel(blocks, ahead, x_ref, gain_ref, weight_refs, *scratch):
    x_buf, weight_buf, rope_buf, scaled_ref, total_ref, square_ref, sems = scratch
    rows, width = x_ref.shape
    copies = []
    ends = [sum(blocks[: k + 1]) for k in range(len(blocks))]
    for k, (size, end) in enumerate(zip(blocks, ends)):
        part = pl.ds(end - size, size)
        group = [pltpu.make_async_copy(x_ref.at[:, part], x_buf.at[:, part], sems.at[0, k])]
        first = 0
        for i, weight_ref in enumerate(weight_refs):
            to = weight_buf.at[part, pl.ds(first, weight_ref.shape[1])]
            group.append(pltpu.make_async_copy(weight_ref.at[part, :], to, sems.at[1 + i, k]))
            first += weight_ref.shape[1]
        copies.append(group)
    for pair in copies[:ahead]:
        for copy in pair:
            copy.start()
    rope_factors(rope_buf, lax.axis_index("seq") * rows)
    chunk = 64
    for k, (size, end) in enumerate(zip(blocks, ends)):
        for copy in copies[k]:
            copy.wait()
        if k + ahead < len(blocks):
            for copy in copies[k + ahead]:
                copy.start()
        for r in range(0, rows, chunk):
            part = None
            for t in range(end - size, end, LANES):
                x = x_buf[r : r + chunk, t : t + LANES]
                gain = gain_ref[t // LANES : t // LANES + 1, :].astype(BF16)
                scaled_ref[r : r + chunk, t : t + LANES] = x * gain
                square = x * x
                part = square if part is None else part + square
            part = part.astype(F32)
            square_ref[r : r + chunk, :] = part if k == 0 else square_ref[r : r + chunk, :] + part
        span = slice(end - size, end)
        product = matmul(scaled_ref[:, span], weight_buf[span, :])
        total_ref[...] = product if k == 0 else total_ref[...] + product
    mean = jnp.sum(square_ref[...], axis=1, keepdims=True) * (1.0 / width)
    return lax.rsqrt(mean + 1e-06)


def project_all_kernel(scale, width, mp, blocks, ahead, cut, x_ref, gain_ref, *refs):
    kv_weight_ref, query_weight_ref, out_weight_ref, *refs = refs
    queries_ref, kv_ref, *refs = refs
    pieces, scratch, cut_sems = refs[: len(cut)], refs[len(cut) : -1], refs[-1]
    copies = cut_copies(width, mp, cut, out_weight_ref, pieces, cut_sems)
    for copy in copies:
        copy.start()
    weights = (kv_weight_ref, query_weight_ref)
    inverse = project_kernel(blocks, ahead, x_ref, gain_ref, weights, *scratch)
    rope_buf, total_ref = scratch[2], scratch[4]
    rows, head = queries_ref.shape
    cosine, sine = rope_buf[0], rope_buf[1]
    kv_ref[:rows, :] = rope(total_ref[:, :head] * inverse, cosine, sine).astype(BF16)
    for t in range(rows // LANES):
        span = slice(t * LANES, (t + 1) * LANES)
        values = total_ref[span, head : 2 * head] * inverse[span, :]
        kv_ref[rows + t * head : rows + (t + 1) * head, :] = values.T.astype(BF16)
    queries = rope(total_ref[:, 2 * head :] * (inverse * scale), cosine, sine)
    queries_ref[...] = queries.astype(BF16)
    for copy in copies:
        copy.wait()


BLOCKS = (1280, 1280, 1280, 1024, 512)
AHEAD = 4
MIXED_COST = 10**11


def project_scratch(rows, width, cols, head):
    return [
        pltpu.VMEM((rows, width), BF16),
        pltpu.VMEM((width, cols), BF16),
        pltpu.VMEM((2, rows, head), F32),
        pltpu.VMEM((rows, width), BF16),
        pltpu.VMEM((rows, cols), F32),
        pltpu.VMEM((rows, LANES), F32),
        pltpu.SemaphoreType.DMA((3, len(BLOCKS))),
    ]


def values_of(block_ref, start):
    head = block_ref.shape[1]
    tiles = [block_ref[r : r + head, :] for r in range(start, block_ref.shape[0], head)]
    return jnp.concatenate(tiles, axis=1)


def pass_kernel(own_ref, far_ref, keys_ref, values_ref):
    core = lax.axis_index("seq") % 2
    rows = keys_ref.shape[0]
    keys_ref[...] = jnp.where(core == 0, own_ref[:rows, :], far_ref[:rows, :])
    values_ref[...] = jnp.where(core == 0, own_ref[rows:, :], far_ref[rows:, :])


NT = ((1,), (1,))


def mixed_kernel(q_ref, own_ref, far_ref, out_ref, stats_ref):
    rows = q_ref.shape[0]
    chunk = min(rows, 256)
    bias = jnp.where(lax.axis_index("seq") < 2, MASKED, 0.0).astype(F32)
    own_values, far_values = values_of(own_ref, rows), values_of(far_ref, rows)
    for start in range(0, rows, chunk):
        span = slice(start, start + chunk)
        q = q_ref[span, :]
        key_index = lax.broadcasted_iota(jnp.int32, (rows, chunk), 0)
        query_index = lax.broadcasted_iota(jnp.int32, (rows, chunk), 1) + start
        own = key_index <= query_index
        far = matmul(far_ref[:rows, :], q, NT) + bias
        scores = jnp.where(own, matmul(own_ref[:rows, :], q, NT), far)
        highest = jnp.max(scores, axis=0, keepdims=True)
        expo = jnp.exp2(scores - highest)
        stats_ref[0:1, span] = highest
        stats_ref[1:2, span] = jnp.sum(expo, axis=0, keepdims=True)
        out = matmul(own_values, jnp.where(own, expo, 0.0).astype(BF16))
        out_ref[:, span] = out + matmul(far_values, jnp.where(own, 0.0, expo).astype(BF16))


def near_kernel(q_ref, keys_ref, values_ref, mixed_ref, stats_ref, out_ref):
    rows = q_ref.shape[0]
    chunk = min(rows, 256)
    bias = jnp.where(lax.axis_index("seq") < 1, MASKED, 0.0).astype(F32)
    values = values_of(values_ref, 0)
    for start in range(0, rows, chunk):
        span = slice(start, start + chunk)
        scores = matmul(keys_ref[...], q_ref[span, :], NT) + bias
        before = stats_ref[0:1, span]
        highest = jnp.maximum(before, jnp.max(scores, axis=0, keepdims=True))
        expo = jnp.exp2(scores - highest)
        scale = jnp.exp2(before - highest)
        norm = stats_ref[1:2, span] * scale + jnp.sum(expo, axis=0, keepdims=True)
        out = mixed_ref[:, span] * scale + matmul(values, expo.astype(BF16))
        out_ref[:, span] = (out * (1.0 / norm)).astype(BF16)


def weight_window(width, mp):
    cols = width // mp
    tiles = max(-(-cols * (m + 1) // LANES) - cols * m // LANES for m in range(mp))
    return cols, tiles


def window_start(m, width, mp):
    cols, tiles = weight_window(width, mp)
    first = jnp.minimum(m * cols // LANES, width // LANES - tiles)
    return first * LANES


def cut_copies(width, mp, distances, weight_ref, outs, sems):
    m = lax.axis_index("mp")
    place = lax.axis_index("seq")
    half = weight_ref.shape[0] // 2
    copies = []
    for i, (distance, out) in enumerate(zip(distances, outs)):
        count, window = out.shape
        row = place % 2 * half + place // 2 % 2 * (half - count)
        start = window_start(partner(m, distance, mp), width, mp)
        source = weight_ref.at[
            pl.ds(pl.multiple_of(row, 16), count), pl.ds(pl.multiple_of(start, LANES), window)
        ]
        copies.append(pltpu.make_async_copy(source, out, sems.at[i]))
    return copies


def turn_kernel(width, mp, split, *refs):
    pieces, (weight_ref, out_ref, own_ref, sem) = list(refs[:-5]), refs[-4:]
    half, window = own_ref.shape
    (copy,) = cut_copies(width, mp, [0], weight_ref, [own_ref], sem)
    copy.start()
    chip = lax.axis_index("seq") // 2 % 2
    copy.wait()
    blocks = {-1: own_ref[...]}
    for i in sorted(range(mp - 1), key=lambda i: not split[i]):
        block = pieces.pop(0)[...]
        if split[i]:
            other = pieces.pop(0)[...]
            low = jnp.where(chip == 0, block, other)
            high = jnp.where(chip == 0, other, block)
            block = jnp.concatenate([low, high], axis=0)
        blocks[i] = block
    for i in range(0, mp, 2):
        pair = jnp.concatenate([blocks[i - 1], blocks[i]], axis=0)
        out_ref[:, i * half : (i + 2) * half] = pair.T


def collect_kernel(pairs, *refs):
    heads, out_ref = refs[:-1], refs[-1]
    head, rows = heads[0].shape
    half = head // 2
    core = lax.axis_index("seq") % 2
    for place in range(2):
        row = pl.multiple_of((core if place == 0 else 1 - core) * half, half)
        for i in range(pairs):
            to = (place * pairs + i) * half
            if i < len(heads):
                out_ref[to : to + half, :] = heads[i][pl.ds(row, half), :]
            else:
                out_ref[to : to + half, :] = jnp.zeros((half, rows), BF16)


def first_heads_kernel(mine_ref, theirs_ref, heads_ref, out_ref):
    half = mine_ref.shape[1]
    chunk = max(c for c in range(16, 513, 16) if mine_ref.shape[0] % c == 0)
    for start in range(0, mine_ref.shape[0], chunk):
        span = slice(start, start + chunk)
        total = matmul(mine_ref[span, :], heads_ref[:half, :])
        out_ref[span, :] = total + matmul(theirs_ref[span, :], heads_ref[half:, :])


def output_kernel(width, mp, chunk, mine_ref, theirs_ref, first_ref, last_ref, *refs):
    out_ref, heads_ref, buf_ref, sems = refs
    cols = out_ref.shape[0]
    head = last_ref.shape[0]
    half = head // 2
    m = lax.axis_index("mp")
    offset = m * cols - window_start(m, width, mp)
    core = lax.axis_index("seq") % 2
    heads_ref[...] = jnp.zeros_like(heads_ref)
    for place in range(2):
        row = pl.multiple_of((core if place == 0 else 1 - core) * half, half)
        heads_ref[place * head + half : (place + 1) * head, :] = last_ref[pl.ds(row, half), :]
    copies = []
    for i in range(cols // chunk):
        span = pl.ds(i * chunk, chunk)
        rows = pl.ds(pl.multiple_of(offset + i * chunk, 16), chunk)
        weight = jnp.concatenate([mine_ref[rows, -LANES:], theirs_ref[rows, -LANES:]], axis=1)
        total = first_ref[rows, :] + matmul(weight, heads_ref[...])
        buf_ref[span, :] = total.astype(BF16)
        copies.append(pltpu.make_async_copy(buf_ref.at[span, :], out_ref.at[span, :], sems.at[i]))
        copies[-1].start()
    for copy in copies:
        copy.wait()


def per_device(hidden_in, norm_gain, query_weight, kv_weight, out_weight):
    rows, width = hidden_in.shape
    head = query_weight.shape[1]
    mp = lax.axis_size("mp")
    assert 2 * rows == WINDOW and width == sum(BLOCKS) and head == LANES
    cols, tiles = weight_window(width, mp)
    window = tiles * LANES
    half = head // 2
    gain = norm_gain.reshape(width // LANES, LANES)
    anywhere = pl.BlockSpec(memory_space=pl.ANY)
    hbm = pl.BlockSpec(memory_space=pltpu.HBM)
    vmem = pl.BlockSpec(memory_space=pltpu.VMEM)
    dma = pltpu.SemaphoreType.DMA
    shape = lambda *dims: jax.ShapeDtypeStruct(dims, BF16)
    large = 52 * 2**20

    order = [2, 1, 3] if mp == 4 else list(range(1, mp))
    split = [mp == 4 and d > 1 for d in order]
    counts = [half // 2 if in_two else half for in_two in split]
    scale = math.log2(math.e) / math.sqrt(168.0)
    queries, kv, *pieces = call(
        functools.partial(project_all_kernel, scale, width, mp, BLOCKS, AHEAD, order),
        "project",
        [shape(rows, head), shape(2 * rows, head)] + [shape(c, window) for c in counts],
        vmem=large,
        in_specs=[hbm, vmem, hbm, hbm, hbm],
        out_specs=[vmem] * (2 + len(order)),
        scratch_shapes=project_scratch(rows, width, 3 * head, head) + [dma((len(order),))],
    )(hidden_in, gain, kv_weight, query_weight, out_weight)
    far = around(kv, "seq", 2)
    mine = [exchanged(piece, d) for d, piece in zip(order, pieces)]
    passed = call(
        pass_kernel,
        "pass_on",
        [shape(rows, head), shape(rows, head)],
        in_specs=[vmem] * 2,
        out_specs=[vmem] * 2,
    )(kv, far)
    near = [other_core(block) for block in passed]
    mixed, stats = call(
        mixed_kernel,
        "mixed_blocks",
        [jax.ShapeDtypeStruct((head, rows), F32), jax.ShapeDtypeStruct((2, rows), F32)],
        flops=MIXED_COST,
        in_specs=[vmem] * 3,
        out_specs=[vmem] * 2,
    )(queries, kv, far)
    head_out = call(
        near_kernel,
        "near_block",
        shape(head, rows),
        in_specs=[vmem] * 5,
        out_specs=vmem,
    )(queries, *near, mixed, stats)
    heads = [head_out] + [exchanged(head_out, d) for d in order[:-1]]
    if mp == 4:
        last_head = exchanged(heads[1], 1)
    else:
        last_head = exchanged(head_out, order[-1])

    parts = []
    for i in sorted(range(mp - 1), key=lambda i: not split[i]):
        parts += [mine[i], next_chip(mine[i])] if split[i] else [mine[i]]
    mine_turned = call(
        functools.partial(turn_kernel, width, mp, split),
        "turn_weight",
        shape(window, mp * half),
        in_specs=[vmem] * len(parts) + [anywhere, hbm],
        out_specs=vmem,
        scratch_shapes=[pltpu.VMEM((half, window), BF16), dma((1,))],
    )(*parts, head_out, out_weight)
    theirs_turned = other_core(mine_turned)
    taken = call(
        functools.partial(collect_kernel, mp),
        "collect_heads",
        shape(mp * head, rows),
        flops=3 * 10**10,
        in_specs=[vmem] * (mp - 1),
        out_specs=vmem,
    )(*heads)
    first_sum = call(
        first_heads_kernel,
        "first_heads",
        jax.ShapeDtypeStruct((window, rows), F32),
        in_specs=[vmem] * 3,
        out_specs=vmem,
    )(mine_turned, theirs_turned, taken)

    chunk = max(c for c in range(16, min(cols, 448) + 1, 16) if cols % c == 0)
    return call(
        functools.partial(output_kernel, width, mp, chunk),
        "output",
        shape(cols, rows),
        in_specs=[vmem] * 4,
        out_specs=hbm,
        scratch_shapes=[
            pltpu.VMEM((2 * head, rows), BF16),
            pltpu.VMEM((cols, rows), BF16),
            dma((cols // chunk,)),
        ],
    )(mine_turned, theirs_turned, first_sum, last_head)


def solution(mesh):
    in_specs = (P("seq", None), P(), P(None, "mp"), P(None, "mp"), P("mp", None))
    out_specs = P("mp", "seq")
    return jax.shard_map(
        per_device, mesh=mesh, in_specs=in_specs, out_specs=out_specs, check_vma=False
    )
```

```python
import functools
import math

import jax
import jax.numpy as jnp
import numpy as np
from jax import lax
from jax.experimental import pallas as pl
from jax.experimental.pallas import tpu as pltpu
from jax.sharding import PartitionSpec as P

WINDOW = 1024
LANES = 128
MASKED = -1e30
F32 = jnp.float32
BF16 = jnp.bfloat16


def around(block, axis, distance):
    size = lax.axis_size(axis)
    return lax.ppermute(block, axis, [(i, (i + distance) % size) for i in range(size)])


def other_core(block):
    return lax.ppermute(block, "seq", [(i, i ^ 1) for i in range(lax.axis_size("seq"))])


def next_chip(block):
    return lax.ppermute(block, "seq", [(i, i ^ 2) for i in range(lax.axis_size("seq"))])


def partner(m, distance, mp):
    return m ^ distance if mp == 4 else (m + distance) % mp


def exchanged(block, distance):
    mp = lax.axis_size("mp")
    return lax.ppermute(block, "mp", [(i, partner(i, distance, mp)) for i in range(mp)])


def call(kernel, name, out_shape, vmem=16 * 2**20, flops=1, **kwargs):
    return pl.pallas_call(
        kernel,
        name=name,
        out_shape=out_shape,
        cost_estimate=pl.CostEstimate(flops=flops, bytes_accessed=1, transcendentals=0),
        compiler_params=pltpu.CompilerParams(vmem_limit_bytes=vmem),
        **kwargs,
    )


def matmul(left, right, dims=((1,), (0,))):
    return lax.dot_general(left, right, (dims, ((), ())), preferred_element_type=F32)


def rope_factors(rope_ref, first_pos):
    rows, head = rope_ref.shape[1:]
    half = head // 2
    step = 8

    def turn(count, stride, start):
        lane = lax.broadcasted_iota(jnp.int32, (count, head), 1)
        low = lane < half
        freq = jnp.exp(
            jnp.where(low, lane, lane - half).astype(F32) * (-math.log(10000.0) * 2.0 / head)
        )
        place = lax.broadcasted_iota(jnp.int32, (count, head), 0) * stride + start
        angle = place.astype(F32) * freq
        return jnp.cos(angle), jnp.sin(angle), jnp.where(low, -1.0, 1.0)

    fine_cos, fine_sin, _ = turn(step, 1, 0)
    coarse_cos, coarse_sin, sign = turn(rows // step, step, first_pos)
    for a in range(rows // step):
        span = slice(a * step, (a + 1) * step)
        c, s = coarse_cos[a : a + 1, :], coarse_sin[a : a + 1, :]
        rope_ref[0, span, :] = c * fine_cos - s * fine_sin
        rope_ref[1, span, :] = (s * fine_cos + c * fine_sin) * sign[:step, :]


def rope(tensor, cosine, sine):
    return tensor * cosine + pltpu.roll(tensor, tensor.shape[1] // 2, 1) * sine


def project_kernel(blocks, ahead, x_ref, gain_ref, weight_refs, *scratch):
    x_buf, weight_buf, rope_buf, scaled_ref, total_ref, square_ref, sems = scratch
    rows, width = x_ref.shape
    copies = []
    ends = [sum(blocks[: k + 1]) for k in range(len(blocks))]
    for k, (size, end) in enumerate(zip(blocks, ends)):
        part = pl.ds(end - size, size)
        group = [pltpu.make_async_copy(x_ref.at[:, part], x_buf.at[:, part], sems.at[0, k])]
        first = 0
        for i, weight_ref in enumerate(weight_refs):
            to = weight_buf.at[part, pl.ds(first, weight_ref.shape[1])]
            group.append(pltpu.make_async_copy(weight_ref.at[part, :], to, sems.at[1 + i, k]))
            first += weight_ref.shape[1]
        copies.append(group)
    for pair in copies[:ahead]:
        for copy in pair:
            copy.start()
    rope_factors(rope_buf, lax.axis_index("seq") * rows)
    chunk = 64
    for k, (size, end) in enumerate(zip(blocks, ends)):
        for copy in copies[k]:
            copy.wait()
        if k + ahead < len(blocks):
            for copy in copies[k + ahead]:
                copy.start()
        for r in range(0, rows, chunk):
            part = None
            for t in range(end - size, end, LANES):
                x = x_buf[r : r + chunk, t : t + LANES]
                gain = gain_ref[t // LANES : t // LANES + 1, :].astype(BF16)
                scaled_ref[r : r + chunk, t : t + LANES] = x * gain
                square = x * x
                part = square if part is None else part + square
            part = part.astype(F32)
            square_ref[r : r + chunk, :] = part if k == 0 else square_ref[r : r + chunk, :] + part
        span = slice(end - size, end)
        product = matmul(scaled_ref[:, span], weight_buf[span, :])
        total_ref[...] = product if k == 0 else total_ref[...] + product
    mean = jnp.sum(square_ref[...], axis=1, keepdims=True) * (1.0 / width)
    return lax.rsqrt(mean + 1e-06)


def project_all_kernel(scale, width, mp, blocks, ahead, cut, x_ref, gain_ref, *refs):
    kv_weight_ref, query_weight_ref, out_weight_ref, *refs = refs
    queries_ref, kv_ref, *refs = refs
    pieces, scratch, cut_sems = refs[: len(cut)], refs[len(cut) : -1], refs[-1]
    copies = cut_copies(width, mp, cut, out_weight_ref, pieces, cut_sems)
    for copy in copies:
        copy.start()
    weights = (kv_weight_ref, query_weight_ref)
    inverse = project_kernel(blocks, ahead, x_ref, gain_ref, weights, *scratch)
    rope_buf, total_ref = scratch[2], scratch[4]
    rows, head = queries_ref.shape
    cosine, sine = rope_buf[0], rope_buf[1]
    kv_ref[:rows, :] = rope(total_ref[:, :head] * inverse, cosine, sine).astype(BF16)
    for t in range(rows // LANES):
        span = slice(t * LANES, (t + 1) * LANES)
        values = total_ref[span, head : 2 * head] * inverse[span, :]
        kv_ref[rows + t * head : rows + (t + 1) * head, :] = values.T.astype(BF16)
    queries = rope(total_ref[:, 2 * head :] * (inverse * scale), cosine, sine)
    queries_ref[...] = queries.astype(BF16)
    for copy in copies:
        copy.wait()


BLOCKS = (1280, 1280, 1280, 1024, 512)
AHEAD = 4
MIXED_COST = 10**11


def project_scratch(rows, width, cols, head):
    return [
        pltpu.VMEM((rows, width), BF16),
        pltpu.VMEM((width, cols), BF16),
        pltpu.VMEM((2, rows, head), F32),
        pltpu.VMEM((rows, width), BF16),
        pltpu.VMEM((rows, cols), F32),
        pltpu.VMEM((rows, LANES), F32),
        pltpu.SemaphoreType.DMA((3, len(BLOCKS))),
    ]


def values_of(block_ref, start):
    head = block_ref.shape[1]
    tiles = [block_ref[r : r + head, :] for r in range(start, block_ref.shape[0], head)]
    return jnp.concatenate(tiles, axis=1)


def pass_kernel(own_ref, far_ref, out_ref):
    core = lax.axis_index("seq") % 2
    out_ref[...] = jnp.where(core == 0, own_ref[...], far_ref[...])


NT = ((1,), (1,))


def mixed_kernel(q_ref, own_ref, far_ref, out_ref, stats_ref):
    rows = q_ref.shape[0]
    chunk = rows
    bias = jnp.where(lax.axis_index("seq") < 2, MASKED, 0.0).astype(F32)
    own_values, far_values = values_of(own_ref, rows), values_of(far_ref, rows)
    for start in range(0, rows, chunk):
        span = slice(start, start + chunk)
        q = q_ref[span, :]
        key_index = lax.broadcasted_iota(jnp.int32, (rows, chunk), 0)
        query_index = lax.broadcasted_iota(jnp.int32, (rows, chunk), 1) + start
        own = key_index <= query_index
        far = matmul(far_ref[:rows, :], q, NT) + bias
        scores = jnp.where(own, matmul(own_ref[:rows, :], q, NT), far)
        highest = jnp.max(scores, axis=0, keepdims=True)
        expo = jnp.exp2(scores - highest)
        stats_ref[0:1, span] = highest
        stats_ref[1:2, span] = jnp.sum(expo, axis=0, keepdims=True)
        out = matmul(own_values, jnp.where(own, expo, 0.0).astype(BF16))
        out_ref[:, span] = out + matmul(far_values, jnp.where(own, 0.0, expo).astype(BF16))


def near_kernel(q_ref, near_ref, mixed_ref, stats_ref, out_ref):
    rows = q_ref.shape[0]
    chunk = rows
    bias = jnp.where(lax.axis_index("seq") < 1, MASKED, 0.0).astype(F32)
    values = values_of(near_ref, rows)
    for start in range(0, rows, chunk):
        span = slice(start, start + chunk)
        scores = matmul(near_ref[:rows, :], q_ref[span, :], NT) + bias
        before = stats_ref[0:1, span]
        highest = jnp.maximum(before, jnp.max(scores, axis=0, keepdims=True))
        expo = jnp.exp2(scores - highest)
        scale = jnp.exp2(before - highest)
        norm = stats_ref[1:2, span] * scale + jnp.sum(expo, axis=0, keepdims=True)
        out = mixed_ref[:, span] * scale + matmul(values, expo.astype(BF16))
        out_ref[:, span] = (out * (1.0 / norm)).astype(BF16)


def weight_window(width, mp):
    cols = width // mp
    tiles = max(-(-cols * (m + 1) // LANES) - cols * m // LANES for m in range(mp))
    return cols, tiles


def window_start(m, width, mp):
    cols, tiles = weight_window(width, mp)
    first = jnp.minimum(m * cols // LANES, width // LANES - tiles)
    return first * LANES


def cut_copies(width, mp, distances, weight_ref, outs, sems):
    m = lax.axis_index("mp")
    place = lax.axis_index("seq")
    half = weight_ref.shape[0] // 2
    copies = []
    for i, (distance, out) in enumerate(zip(distances, outs)):
        count, window = out.shape
        row = place % 2 * half + place // 2 % 2 * (half - count)
        start = window_start(partner(m, distance, mp), width, mp)
        source = weight_ref.at[
            pl.ds(pl.multiple_of(row, 16), count), pl.ds(pl.multiple_of(start, LANES), window)
        ]
        copies.append(pltpu.make_async_copy(source, out, sems.at[i]))
    return copies


def turn_kernel(width, mp, split, sequence, *refs):
    pieces, (weight_ref, out_ref, own_ref, sem) = list(refs[:-5]), refs[-4:]
    half, window = own_ref.shape
    (copy,) = cut_copies(width, mp, [0], weight_ref, [own_ref], sem)
    copy.start()
    chip = lax.axis_index("seq") // 2 % 2
    copy.wait()
    blocks = {-1: own_ref[...]}
    for i in sequence:
        block = pieces.pop(0)[...]
        if split[i]:
            other = pieces.pop(0)[...]
            low = jnp.where(chip == 0, block, other)
            high = jnp.where(chip == 0, other, block)
            block = jnp.concatenate([low, high], axis=0)
        blocks[i] = block
    for i in range(0, mp, 2):
        pair = jnp.concatenate([blocks[i - 1], blocks[i]], axis=0)
        out_ref[:, i * half : (i + 2) * half] = pair.T


def collect_kernel(pairs, *refs):
    heads, out_ref = refs[:-1], refs[-1]
    head, rows = heads[0].shape
    half = head // 2
    core = lax.axis_index("seq") % 2
    for place in range(2):
        row = pl.multiple_of((core if place == 0 else 1 - core) * half, half)
        for i in range(pairs):
            to = (place * pairs + i) * half
            if i < len(heads):
                out_ref[to : to + half, :] = heads[i][pl.ds(row, half), :]
            else:
                out_ref[to : to + half, :] = jnp.zeros((half, rows), BF16)


def first_heads_kernel(mine_ref, theirs_ref, heads_ref, out_ref):
    half = mine_ref.shape[1]
    chunk = max(c for c in range(16, 513, 16) if mine_ref.shape[0] % c == 0)
    for start in range(0, mine_ref.shape[0], chunk):
        span = slice(start, start + chunk)
        total = matmul(mine_ref[span, :], heads_ref[:half, :])
        out_ref[span, :] = total + matmul(theirs_ref[span, :], heads_ref[half:, :])


def output_kernel(width, mp, chunk, mine_ref, theirs_ref, first_ref, last_ref, *refs):
    out_ref, heads_ref, buf_ref, sems = refs
    cols = out_ref.shape[0]
    head = last_ref.shape[0]
    half = head // 2
    m = lax.axis_index("mp")
    offset = m * cols - window_start(m, width, mp)
    core = lax.axis_index("seq") % 2
    heads_ref[...] = jnp.zeros_like(heads_ref)
    for place in range(2):
        row = pl.multiple_of((core if place == 0 else 1 - core) * half, half)
        heads_ref[place * head + half : (place + 1) * head, :] = last_ref[pl.ds(row, half), :]
    copies = []
    for i in range(cols // chunk):
        span = pl.ds(i * chunk, chunk)
        rows = pl.ds(pl.multiple_of(offset + i * chunk, 16), chunk)
        weight = jnp.concatenate([mine_ref[rows, -LANES:], theirs_ref[rows, -LANES:]], axis=1)
        total = first_ref[rows, :] + matmul(weight, heads_ref[...])
        buf_ref[span, :] = total.astype(BF16)
        copies.append(pltpu.make_async_copy(buf_ref.at[span, :], out_ref.at[span, :], sems.at[i]))
        copies[-1].start()
    for copy in copies:
        copy.wait()


def per_device(hidden_in, norm_gain, query_weight, kv_weight, out_weight):
    rows, width = hidden_in.shape
    head = query_weight.shape[1]
    mp = lax.axis_size("mp")
    assert 2 * rows == WINDOW and width == sum(BLOCKS) and head == LANES
    cols, tiles = weight_window(width, mp)
    window = tiles * LANES
    half = head // 2
    gain = norm_gain.reshape(width // LANES, LANES)
    anywhere = pl.BlockSpec(memory_space=pl.ANY)
    hbm = pl.BlockSpec(memory_space=pltpu.HBM)
    vmem = pl.BlockSpec(memory_space=pltpu.VMEM)
    dma = pltpu.SemaphoreType.DMA
    shape = lambda *dims: jax.ShapeDtypeStruct(dims, BF16)
    large = 52 * 2**20

    order = [3, 1, 2] if mp == 4 else list(range(1, mp))
    split = [mp == 4 and d == 2 for d in order]
    counts = [half // 2 if in_two else half for in_two in split]
    scale = math.log2(math.e) / math.sqrt(168.0)
    queries, kv, *pieces = call(
        functools.partial(project_all_kernel, scale, width, mp, BLOCKS, AHEAD, order),
        "project",
        [shape(rows, head), shape(2 * rows, head)] + [shape(c, window) for c in counts],
        vmem=large,
        in_specs=[hbm, vmem, hbm, hbm, hbm],
        out_specs=[vmem] * (2 + len(order)),
        scratch_shapes=project_scratch(rows, width, 3 * head, head) + [dma((len(order),))],
    )(hidden_in, gain, kv_weight, query_weight, out_weight)
    far = around(kv, "seq", 2)
    mine = [exchanged(piece, d) for d, piece in zip(order, pieces)]
    passed = call(
        pass_kernel,
        "pass_on",
        shape(*kv.shape),
        in_specs=[vmem] * 2,
        out_specs=vmem,
    )(kv, far)
    near = other_core(passed)
    mixed, stats = call(
        mixed_kernel,
        "mixed_blocks",
        [jax.ShapeDtypeStruct((head, rows), F32), jax.ShapeDtypeStruct((2, rows), F32)],
        flops=MIXED_COST,
        in_specs=[vmem] * 3,
        out_specs=[vmem] * 2,
    )(queries, kv, far)
    head_out = call(
        near_kernel,
        "near_block",
        shape(head, rows),
        in_specs=[vmem] * 4,
        out_specs=vmem,
    )(queries, near, mixed, stats)
    heads = [head_out] + [exchanged(head_out, d) for d in order[:-1]]
    if mp == 4:
        last_head = exchanged(heads[1], 1)
    else:
        last_head = exchanged(head_out, order[-1])

    parts = []
    sequence = sorted(range(mp - 1), key=lambda i: (not split[i], -order[i]))
    for i in sequence:
        parts += [mine[i], next_chip(mine[i])] if split[i] else [mine[i]]
    mine_turned = call(
        functools.partial(turn_kernel, width, mp, split, sequence),
        "turn_weight",
        shape(window, mp * half),
        in_specs=[vmem] * len(parts) + [anywhere, hbm],
        out_specs=vmem,
        scratch_shapes=[pltpu.VMEM((half, window), BF16), dma((1,))],
    )(*parts, head_out, out_weight)
    theirs_turned = other_core(mine_turned)
    taken = call(
        functools.partial(collect_kernel, mp),
        "collect_heads",
        shape(mp * head, rows),
        flops=3 * 10**10,
        in_specs=[vmem] * (mp - 1),
        out_specs=vmem,
    )(*heads)
    first_sum = call(
        first_heads_kernel,
        "first_heads",
        jax.ShapeDtypeStruct((window, rows), F32),
        in_specs=[vmem] * 3,
        out_specs=vmem,
    )(mine_turned, theirs_turned, taken)

    chunk = max(c for c in range(16, min(cols, 448) + 1, 16) if cols % c == 0)
    return call(
        functools.partial(output_kernel, width, mp, chunk),
        "output",
        shape(cols, rows),
        in_specs=[vmem] * 4,
        out_specs=hbm,
        scratch_shapes=[
            pltpu.VMEM((2 * head, rows), BF16),
            pltpu.VMEM((cols, rows), BF16),
            dma((cols // chunk,)),
        ],
    )(mine_turned, theirs_turned, first_sum, last_head)


def solution(mesh):
    in_specs = (P("seq", None), P(), P(None, "mp"), P(None, "mp"), P("mp", None))
    out_specs = P("mp", "seq")
    return jax.shard_map(
        per_device, mesh=mesh, in_specs=in_specs, out_specs=out_specs, check_vma=False
    )
```

```python
import functools
import math

import jax
import jax.numpy as jnp
import numpy as np
from jax import lax
from jax.experimental import pallas as pl
from jax.experimental.pallas import tpu as pltpu
from jax.sharding import PartitionSpec as P

WINDOW = 1024
LANES = 128
MASKED = -1e30
F32 = jnp.float32
BF16 = jnp.bfloat16


def around(block, axis, distance):
    size = lax.axis_size(axis)
    return lax.ppermute(block, axis, [(i, (i + distance) % size) for i in range(size)])


def other_core(block):
    return lax.ppermute(block, "seq", [(i, i ^ 1) for i in range(lax.axis_size("seq"))])


def next_chip(block):
    return lax.ppermute(block, "seq", [(i, i ^ 2) for i in range(lax.axis_size("seq"))])


def partner(m, distance, mp):
    return m ^ distance if mp == 4 else (m + distance) % mp


def exchanged(block, distance):
    mp = lax.axis_size("mp")
    return lax.ppermute(block, "mp", [(i, partner(i, distance, mp)) for i in range(mp)])


def call(kernel, name, out_shape, vmem=16 * 2**20, flops=1, **kwargs):
    return pl.pallas_call(
        kernel,
        name=name,
        out_shape=out_shape,
        cost_estimate=pl.CostEstimate(flops=flops, bytes_accessed=1, transcendentals=0),
        compiler_params=pltpu.CompilerParams(vmem_limit_bytes=vmem),
        **kwargs,
    )


def matmul(left, right, dims=((1,), (0,))):
    return lax.dot_general(left, right, (dims, ((), ())), preferred_element_type=F32)


def rope_factors(rope_ref, first_pos):
    rows, head = rope_ref.shape[1:]
    half = head // 2
    step = 8

    def turn(count, stride, start):
        lane = lax.broadcasted_iota(jnp.int32, (count, head), 1)
        low = lane < half
        freq = jnp.exp(
            jnp.where(low, lane, lane - half).astype(F32) * (-math.log(10000.0) * 2.0 / head)
        )
        place = lax.broadcasted_iota(jnp.int32, (count, head), 0) * stride + start
        angle = place.astype(F32) * freq
        return jnp.cos(angle), jnp.sin(angle), jnp.where(low, -1.0, 1.0)

    fine_cos, fine_sin, _ = turn(step, 1, 0)
    coarse_cos, coarse_sin, sign = turn(rows // step, step, first_pos)
    for a in range(rows // step):
        span = slice(a * step, (a + 1) * step)
        c, s = coarse_cos[a : a + 1, :], coarse_sin[a : a + 1, :]
        rope_ref[0, span, :] = c * fine_cos - s * fine_sin
        rope_ref[1, span, :] = (s * fine_cos + c * fine_sin) * sign[:step, :]


def rope(tensor, cosine, sine):
    return tensor * cosine + pltpu.roll(tensor, tensor.shape[1] // 2, 1) * sine


def project_kernel(blocks, ahead, x_ref, gain_ref, weight_refs, *scratch):
    x_buf, weight_buf, rope_buf, scaled_ref, total_ref, square_ref, sems = scratch
    rows, width = x_ref.shape
    copies = []
    ends = [sum(blocks[: k + 1]) for k in range(len(blocks))]
    for k, (size, end) in enumerate(zip(blocks, ends)):
        part = pl.ds(end - size, size)
        group = [pltpu.make_async_copy(x_ref.at[:, part], x_buf.at[:, part], sems.at[0, k])]
        first = 0
        for i, weight_ref in enumerate(weight_refs):
            to = weight_buf.at[part, pl.ds(first, weight_ref.shape[1])]
            group.append(pltpu.make_async_copy(weight_ref.at[part, :], to, sems.at[1 + i, k]))
            first += weight_ref.shape[1]
        copies.append(group)
    for pair in copies[:ahead]:
        for copy in pair:
            copy.start()
    rope_factors(rope_buf, lax.axis_index("seq") * rows)
    chunk = 64
    for k, (size, end) in enumerate(zip(blocks, ends)):
        for copy in copies[k]:
            copy.wait()
        if k + ahead < len(blocks):
            for copy in copies[k + ahead]:
                copy.start()
        for r in range(0, rows, chunk):
            part = None
            for t in range(end - size, end, LANES):
                x = x_buf[r : r + chunk, t : t + LANES].astype(F32)
                gain = gain_ref[t // LANES : t // LANES + 1, :]
                scaled_ref[r : r + chunk, t : t + LANES] = (x * gain).astype(BF16)
                square = x * x
                part = square if part is None else part + square
            square_ref[r : r + chunk, :] = part if k == 0 else square_ref[r : r + chunk, :] + part
        span = slice(end - size, end)
        product = matmul(scaled_ref[:, span], weight_buf[span, :])
        total_ref[...] = product if k == 0 else total_ref[...] + product
    mean = jnp.sum(square_ref[...], axis=1, keepdims=True) * (1.0 / width)
    return lax.rsqrt(mean + 1e-06)


def project_all_kernel(scale, width, mp, blocks, ahead, cut, x_ref, gain_ref, *refs):
    kv_weight_ref, query_weight_ref, out_weight_ref, *refs = refs
    queries_ref, kv_ref, *refs = refs
    pieces, scratch, cut_sems = refs[: len(cut)], refs[len(cut) : -1], refs[-1]
    copies = cut_copies(width, mp, cut, out_weight_ref, pieces, cut_sems)
    for copy in copies:
        copy.start()
    weights = (kv_weight_ref, query_weight_ref)
    inverse = project_kernel(blocks, ahead, x_ref, gain_ref, weights, *scratch)
    rope_buf, total_ref = scratch[2], scratch[4]
    rows, head = queries_ref.shape
    cosine, sine = rope_buf[0], rope_buf[1]
    kv_ref[:rows, :] = rope(total_ref[:, :head] * inverse, cosine, sine).astype(BF16)
    for t in range(rows // LANES):
        span = slice(t * LANES, (t + 1) * LANES)
        values = total_ref[span, head : 2 * head] * inverse[span, :]
        kv_ref[rows + t * head : rows + (t + 1) * head, :] = values.T.astype(BF16)
    queries = rope(total_ref[:, 2 * head :] * (inverse * scale), cosine, sine)
    queries_ref[...] = queries.astype(BF16)
    for copy in copies:
        copy.wait()


BLOCKS = (1280, 1280, 1280, 1024, 512)
AHEAD = 4
MIXED_COST = 10**11


def project_scratch(rows, width, cols, head):
    return [
        pltpu.VMEM((rows, width), BF16),
        pltpu.VMEM((width, cols), BF16),
        pltpu.VMEM((2, rows, head), F32),
        pltpu.VMEM((rows, width), BF16),
        pltpu.VMEM((rows, cols), F32),
        pltpu.VMEM((rows, LANES), F32),
        pltpu.SemaphoreType.DMA((3, len(BLOCKS))),
    ]


def values_of(block_ref, start):
    head = block_ref.shape[1]
    tiles = [block_ref[r : r + head, :] for r in range(start, block_ref.shape[0], head)]
    return jnp.concatenate(tiles, axis=1)


def pass_kernel(own_ref, far_ref, out_ref):
    core = lax.axis_index("seq") % 2
    out_ref[...] = jnp.where(core == 0, own_ref[...], far_ref[...])


NT = ((1,), (1,))


def mixed_kernel(q_ref, own_ref, far_ref, out_ref, stats_ref):
    rows = q_ref.shape[0]
    chunk = rows
    bias = jnp.where(lax.axis_index("seq") < 2, MASKED, 0.0).astype(F32)
    own_values, far_values = values_of(own_ref, rows), values_of(far_ref, rows)
    for start in range(0, rows, chunk):
        span = slice(start, start + chunk)
        q = q_ref[span, :]
        key_index = lax.broadcasted_iota(jnp.int32, (rows, chunk), 0)
        query_index = lax.broadcasted_iota(jnp.int32, (rows, chunk), 1) + start
        own = key_index <= query_index
        far = matmul(far_ref[:rows, :], q, NT) + bias
        scores = jnp.where(own, matmul(own_ref[:rows, :], q, NT), far)
        highest = jnp.max(scores, axis=0, keepdims=True)
        expo = jnp.exp2(scores - highest)
        stats_ref[0:1, span] = highest
        stats_ref[1:2, span] = jnp.sum(expo, axis=0, keepdims=True)
        out = matmul(own_values, jnp.where(own, expo, 0.0).astype(BF16))
        out_ref[:, span] = out + matmul(far_values, jnp.where(own, 0.0, expo).astype(BF16))


def near_kernel(q_ref, near_ref, mixed_ref, stats_ref, out_ref):
    rows = q_ref.shape[0]
    chunk = rows
    bias = jnp.where(lax.axis_index("seq") < 1, MASKED, 0.0).astype(F32)
    values = values_of(near_ref, rows)
    for start in range(0, rows, chunk):
        span = slice(start, start + chunk)
        scores = matmul(near_ref[:rows, :], q_ref[span, :], NT) + bias
        before = stats_ref[0:1, span]
        highest = jnp.maximum(before, jnp.max(scores, axis=0, keepdims=True))
        expo = jnp.exp2(scores - highest)
        scale = jnp.exp2(before - highest)
        norm = stats_ref[1:2, span] * scale + jnp.sum(expo, axis=0, keepdims=True)
        out = mixed_ref[:, span] * scale + matmul(values, expo.astype(BF16))
        out_ref[:, span] = (out * (1.0 / norm)).astype(BF16)


def weight_window(width, mp):
    cols = width // mp
    tiles = max(-(-cols * (m + 1) // LANES) - cols * m // LANES for m in range(mp))
    return cols, tiles


def window_start(m, width, mp):
    cols, tiles = weight_window(width, mp)
    first = jnp.minimum(m * cols // LANES, width // LANES - tiles)
    return first * LANES


def cut_copies(width, mp, distances, weight_ref, outs, sems):
    m = lax.axis_index("mp")
    place = lax.axis_index("seq")
    half = weight_ref.shape[0] // 2
    copies = []
    for i, (distance, out) in enumerate(zip(distances, outs)):
        count, window = out.shape
        row = place % 2 * half + place // 2 % 2 * (half - count)
        start = window_start(partner(m, distance, mp), width, mp)
        source = weight_ref.at[
            pl.ds(pl.multiple_of(row, 16), count), pl.ds(pl.multiple_of(start, LANES), window)
        ]
        copies.append(pltpu.make_async_copy(source, out, sems.at[i]))
    return copies


def turn_kernel(width, mp, split, sequence, *refs):
    pieces, (weight_ref, out_ref, own_ref, sem) = list(refs[:-5]), refs[-4:]
    half, window = own_ref.shape
    (copy,) = cut_copies(width, mp, [0], weight_ref, [own_ref], sem)
    copy.start()
    chip = lax.axis_index("seq") // 2 % 2
    copy.wait()
    blocks = {-1: own_ref[...]}
    for i in sequence:
        block = pieces.pop(0)[...]
        if split[i]:
            other = pieces.pop(0)[...]
            low = jnp.where(chip == 0, block, other)
            high = jnp.where(chip == 0, other, block)
            block = jnp.concatenate([low, high], axis=0)
        blocks[i] = block
    for i in range(0, mp, 2):
        pair = jnp.concatenate([blocks[i - 1], blocks[i]], axis=0)
        out_ref[:, i * half : (i + 2) * half] = pair.T


def collect_kernel(pairs, *refs):
    heads, out_ref = refs[:-1], refs[-1]
    head, rows = heads[0].shape
    half = head // 2
    core = lax.axis_index("seq") % 2
    for place in range(2):
        row = pl.multiple_of((core if place == 0 else 1 - core) * half, half)
        for i in range(pairs):
            to = (place * pairs + i) * half
            if i < len(heads):
                out_ref[to : to + half, :] = heads[i][pl.ds(row, half), :]
            else:
                out_ref[to : to + half, :] = jnp.zeros((half, rows), BF16)


def first_heads_kernel(mine_ref, theirs_ref, heads_ref, out_ref):
    half = mine_ref.shape[1]
    chunk = max(c for c in range(16, 513, 16) if mine_ref.shape[0] % c == 0)
    for start in range(0, mine_ref.shape[0], chunk):
        span = slice(start, start + chunk)
        total = matmul(mine_ref[span, :], heads_ref[:half, :])
        out_ref[span, :] = total + matmul(theirs_ref[span, :], heads_ref[half:, :])


def output_kernel(width, mp, chunk, mine_ref, theirs_ref, first_ref, last_ref, *refs):
    out_ref, heads_ref, buf_ref, sems = refs
    cols = out_ref.shape[0]
    head = last_ref.shape[0]
    half = head // 2
    m = lax.axis_index("mp")
    offset = m * cols - window_start(m, width, mp)
    core = lax.axis_index("seq") % 2
    heads_ref[...] = jnp.zeros_like(heads_ref)
    for place in range(2):
        row = pl.multiple_of((core if place == 0 else 1 - core) * half, half)
        heads_ref[place * head + half : (place + 1) * head, :] = last_ref[pl.ds(row, half), :]
    copies = []
    for i in range(cols // chunk):
        span = pl.ds(i * chunk, chunk)
        rows = pl.ds(pl.multiple_of(offset + i * chunk, 16), chunk)
        weight = jnp.concatenate([mine_ref[rows, -LANES:], theirs_ref[rows, -LANES:]], axis=1)
        total = first_ref[rows, :] + matmul(weight, heads_ref[...])
        buf_ref[span, :] = total.astype(BF16)
        copies.append(pltpu.make_async_copy(buf_ref.at[span, :], out_ref.at[span, :], sems.at[i]))
        copies[-1].start()
    for copy in copies:
        copy.wait()


def per_device(hidden_in, norm_gain, query_weight, kv_weight, out_weight):
    rows, width = hidden_in.shape
    head = query_weight.shape[1]
    mp = lax.axis_size("mp")
    assert 2 * rows == WINDOW and width == sum(BLOCKS) and head == LANES
    cols, tiles = weight_window(width, mp)
    window = tiles * LANES
    half = head // 2
    gain = norm_gain.reshape(width // LANES, LANES)
    anywhere = pl.BlockSpec(memory_space=pl.ANY)
    hbm = pl.BlockSpec(memory_space=pltpu.HBM)
    vmem = pl.BlockSpec(memory_space=pltpu.VMEM)
    dma = pltpu.SemaphoreType.DMA
    shape = lambda *dims: jax.ShapeDtypeStruct(dims, BF16)
    large = 52 * 2**20

    order = [3, 1, 2] if mp == 4 else list(range(1, mp))
    split = [mp == 4 and d == 2 for d in order]
    counts = [half // 2 if in_two else half for in_two in split]
    scale = math.log2(math.e) / math.sqrt(168.0)
    queries, kv, *pieces = call(
        functools.partial(project_all_kernel, scale, width, mp, BLOCKS, AHEAD, order),
        "project",
        [shape(rows, head), shape(2 * rows, head)] + [shape(c, window) for c in counts],
        vmem=large,
        in_specs=[hbm, vmem, hbm, hbm, hbm],
        out_specs=[vmem] * (2 + len(order)),
        scratch_shapes=project_scratch(rows, width, 3 * head, head) + [dma((len(order),))],
    )(hidden_in, gain, kv_weight, query_weight, out_weight)
    far = around(kv, "seq", 2)
    mine = [exchanged(piece, d) for d, piece in zip(order, pieces)]
    passed = call(
        pass_kernel,
        "pass_on",
        shape(*kv.shape),
        in_specs=[vmem] * 2,
        out_specs=vmem,
    )(kv, far)
    near = other_core(passed)
    mixed, stats = call(
        mixed_kernel,
        "mixed_blocks",
        [jax.ShapeDtypeStruct((head, rows), F32), jax.ShapeDtypeStruct((2, rows), F32)],
        flops=MIXED_COST,
        in_specs=[vmem] * 3,
        out_specs=[vmem] * 2,
    )(queries, kv, far)
    head_out = call(
        near_kernel,
        "near_block",
        shape(head, rows),
        in_specs=[vmem] * 4,
        out_specs=vmem,
    )(queries, near, mixed, stats)
    heads = [head_out] + [exchanged(head_out, d) for d in order[:-1]]
    if mp == 4:
        last_head = exchanged(heads[1], 1)
    else:
        last_head = exchanged(head_out, order[-1])

    parts = []
    sequence = sorted(range(mp - 1), key=lambda i: (not split[i], -order[i]))
    for i in sequence:
        parts += [mine[i], next_chip(mine[i])] if split[i] else [mine[i]]
    mine_turned = call(
        functools.partial(turn_kernel, width, mp, split, sequence),
        "turn_weight",
        shape(window, mp * half),
        in_specs=[vmem] * len(parts) + [anywhere, hbm],
        out_specs=vmem,
        scratch_shapes=[pltpu.VMEM((half, window), BF16), dma((1,))],
    )(*parts, head_out, out_weight)
    theirs_turned = other_core(mine_turned)
    taken = call(
        functools.partial(collect_kernel, mp),
        "collect_heads",
        shape(mp * head, rows),
        flops=3 * 10**10,
        in_specs=[vmem] * (mp - 1),
        out_specs=vmem,
    )(*heads)
    first_sum = call(
        first_heads_kernel,
        "first_heads",
        jax.ShapeDtypeStruct((window, rows), F32),
        in_specs=[vmem] * 3,
        out_specs=vmem,
    )(mine_turned, theirs_turned, taken)

    chunk = max(c for c in range(16, min(cols, 448) + 1, 16) if cols % c == 0)
    return call(
        functools.partial(output_kernel, width, mp, chunk),
        "output",
        shape(cols, rows),
        in_specs=[vmem] * 4,
        out_specs=hbm,
        scratch_shapes=[
            pltpu.VMEM((2 * head, rows), BF16),
            pltpu.VMEM((cols, rows), BF16),
            dma((cols // chunk,)),
        ],
    )(mine_turned, theirs_turned, first_sum, last_head)


def solution(mesh):
    in_specs = (P("seq", None), P(), P(None, "mp"), P(None, "mp"), P("mp", None))
    out_specs = P("mp", "seq")
    return jax.shard_map(
        per_device, mesh=mesh, in_specs=in_specs, out_specs=out_specs, check_vma=False
    )
```

```python
import functools
import math

import jax
import jax.numpy as jnp
import numpy as np
from jax import lax
from jax.experimental import pallas as pl
from jax.experimental.pallas import tpu as pltpu
from jax.sharding import PartitionSpec as P

WINDOW = 1024
LANES = 128
MASKED = -1e30
F32 = jnp.float32
BF16 = jnp.bfloat16


def around(block, axis, distance):
    size = lax.axis_size(axis)
    return lax.ppermute(block, axis, [(i, (i + distance) % size) for i in range(size)])


def other_core(block):
    return lax.ppermute(block, "seq", [(i, i ^ 1) for i in range(lax.axis_size("seq"))])


def next_chip(block):
    return lax.ppermute(block, "seq", [(i, i ^ 2) for i in range(lax.axis_size("seq"))])


def partner(m, distance, mp):
    return m ^ distance if mp == 4 else (m + distance) % mp


def exchanged(block, distance):
    mp = lax.axis_size("mp")
    return lax.ppermute(block, "mp", [(i, partner(i, distance, mp)) for i in range(mp)])


def call(kernel, name, out_shape, vmem=16 * 2**20, flops=1, **kwargs):
    return pl.pallas_call(
        kernel,
        name=name,
        out_shape=out_shape,
        cost_estimate=pl.CostEstimate(flops=flops, bytes_accessed=1, transcendentals=0),
        compiler_params=pltpu.CompilerParams(vmem_limit_bytes=vmem),
        **kwargs,
    )


def matmul(left, right, dims=((1,), (0,))):
    return lax.dot_general(left, right, (dims, ((), ())), preferred_element_type=F32)


def rope_factors(rope_ref, first_pos):
    rows, head = rope_ref.shape[1:]
    half = head // 2
    step = 8

    def turn(count, stride, start):
        lane = lax.broadcasted_iota(jnp.int32, (count, head), 1)
        low = lane < half
        freq = jnp.exp(
            jnp.where(low, lane, lane - half).astype(F32) * (-math.log(10000.0) * 2.0 / head)
        )
        place = lax.broadcasted_iota(jnp.int32, (count, head), 0) * stride + start
        angle = place.astype(F32) * freq
        return jnp.cos(angle), jnp.sin(angle), jnp.where(low, -1.0, 1.0)

    fine_cos, fine_sin, _ = turn(step, 1, 0)
    coarse_cos, coarse_sin, sign = turn(rows // step, step, first_pos)
    for a in range(rows // step):
        span = slice(a * step, (a + 1) * step)
        c, s = coarse_cos[a : a + 1, :], coarse_sin[a : a + 1, :]
        rope_ref[0, span, :] = c * fine_cos - s * fine_sin
        rope_ref[1, span, :] = (s * fine_cos + c * fine_sin) * sign[:step, :]


def rope(tensor, cosine, sine):
    return tensor * cosine + pltpu.roll(tensor, tensor.shape[1] // 2, 1) * sine


def project_kernel(blocks, ahead, x_ref, gain_ref, weight_refs, *scratch):
    x_buf, weight_buf, rope_buf, scaled_ref, total_ref, square_ref, sems = scratch
    rows, width = x_ref.shape
    copies = []
    ends = [sum(blocks[: k + 1]) for k in range(len(blocks))]
    for k, (size, end) in enumerate(zip(blocks, ends)):
        part = pl.ds(end - size, size)
        group = [pltpu.make_async_copy(x_ref.at[:, part], x_buf.at[:, part], sems.at[0, k])]
        first = 0
        for i, weight_ref in enumerate(weight_refs):
            to = weight_buf.at[part, pl.ds(first, weight_ref.shape[1])]
            group.append(pltpu.make_async_copy(weight_ref.at[part, :], to, sems.at[1 + i, k]))
            first += weight_ref.shape[1]
        copies.append(group)
    for pair in copies[:ahead]:
        for copy in pair:
            copy.start()
    rope_factors(rope_buf, lax.axis_index("seq") * rows)
    chunk = 64
    for k, (size, end) in enumerate(zip(blocks, ends)):
        for copy in copies[k]:
            copy.wait()
        if k + ahead < len(blocks):
            for copy in copies[k + ahead]:
                copy.start()
        for r in range(0, rows, chunk):
            part = None
            for t in range(end - size, end, LANES):
                x = x_buf[r : r + chunk, t : t + LANES]
                gain = gain_ref[t // LANES : t // LANES + 1, :].astype(BF16)
                scaled_ref[r : r + chunk, t : t + LANES] = x * gain
                x = x.astype(F32)
                square = x * x
                part = square if part is None else part + square
            square_ref[r : r + chunk, :] = part if k == 0 else square_ref[r : r + chunk, :] + part
        span = slice(end - size, end)
        product = matmul(scaled_ref[:, span], weight_buf[span, :])
        total_ref[...] = product if k == 0 else total_ref[...] + product
    mean = jnp.sum(square_ref[...], axis=1, keepdims=True) * (1.0 / width)
    return lax.rsqrt(mean + 1e-06)


def project_all_kernel(scale, width, mp, blocks, ahead, cut, x_ref, gain_ref, *refs):
    kv_weight_ref, query_weight_ref, out_weight_ref, *refs = refs
    queries_ref, kv_ref, *refs = refs
    pieces, scratch, cut_sems = refs[: len(cut)], refs[len(cut) : -1], refs[-1]
    copies = cut_copies(width, mp, cut, out_weight_ref, pieces, cut_sems)
    for copy in copies:
        copy.start()
    weights = (kv_weight_ref, query_weight_ref)
    inverse = project_kernel(blocks, ahead, x_ref, gain_ref, weights, *scratch)
    rope_buf, total_ref = scratch[2], scratch[4]
    rows, head = queries_ref.shape
    cosine, sine = rope_buf[0], rope_buf[1]
    kv_ref[:rows, :] = rope(total_ref[:, :head] * inverse, cosine, sine).astype(BF16)
    for t in range(rows // LANES):
        span = slice(t * LANES, (t + 1) * LANES)
        values = total_ref[span, head : 2 * head] * inverse[span, :]
        kv_ref[rows + t * head : rows + (t + 1) * head, :] = values.T.astype(BF16)
    queries = rope(total_ref[:, 2 * head :] * (inverse * scale), cosine, sine)
    queries_ref[...] = queries.astype(BF16)
    for copy in copies:
        copy.wait()


BLOCKS = (1280, 1280, 1280, 1024, 512)
AHEAD = 4
MIXED_COST = 10**11


def project_scratch(rows, width, cols, head):
    return [
        pltpu.VMEM((rows, width), BF16),
        pltpu.VMEM((width, cols), BF16),
        pltpu.VMEM((2, rows, head), F32),
        pltpu.VMEM((rows, width), BF16),
        pltpu.VMEM((rows, cols), F32),
        pltpu.VMEM((rows, LANES), F32),
        pltpu.SemaphoreType.DMA((3, len(BLOCKS))),
    ]


def values_of(block_ref, start):
    head = block_ref.shape[1]
    tiles = [block_ref[r : r + head, :] for r in range(start, block_ref.shape[0], head)]
    return jnp.concatenate(tiles, axis=1)


def pass_kernel(own_ref, far_ref, out_ref):
    core = lax.axis_index("seq") % 2
    out_ref[...] = jnp.where(core == 0, own_ref[...], far_ref[...])


NT = ((1,), (1,))


def mixed_kernel(q_ref, own_ref, far_ref, out_ref, stats_ref):
    rows = q_ref.shape[0]
    chunk = rows
    bias = jnp.where(lax.axis_index("seq") < 2, MASKED, 0.0).astype(F32)
    own_values, far_values = values_of(own_ref, rows), values_of(far_ref, rows)
    for start in range(0, rows, chunk):
        span = slice(start, start + chunk)
        q = q_ref[span, :]
        key_index = lax.broadcasted_iota(jnp.int32, (rows, chunk), 0)
        query_index = lax.broadcasted_iota(jnp.int32, (rows, chunk), 1) + start
        own = key_index <= query_index
        far = matmul(far_ref[:rows, :], q, NT) + bias
        scores = jnp.where(own, matmul(own_ref[:rows, :], q, NT), far)
        highest = jnp.max(scores, axis=0, keepdims=True)
        expo = jnp.exp2(scores - highest)
        stats_ref[0:1, span] = highest
        stats_ref[1:2, span] = jnp.sum(expo, axis=0, keepdims=True)
        out = matmul(own_values, jnp.where(own, expo, 0.0).astype(BF16))
        out_ref[:, span] = out + matmul(far_values, jnp.where(own, 0.0, expo).astype(BF16))


def near_kernel(q_ref, near_ref, mixed_ref, stats_ref, out_ref):
    rows = q_ref.shape[0]
    chunk = rows
    bias = jnp.where(lax.axis_index("seq") < 1, MASKED, 0.0).astype(F32)
    values = values_of(near_ref, rows)
    for start in range(0, rows, chunk):
        span = slice(start, start + chunk)
        scores = matmul(near_ref[:rows, :], q_ref[span, :], NT) + bias
        before = stats_ref[0:1, span]
        highest = jnp.maximum(before, jnp.max(scores, axis=0, keepdims=True))
        expo = jnp.exp2(scores - highest)
        scale = jnp.exp2(before - highest)
        norm = stats_ref[1:2, span] * scale + jnp.sum(expo, axis=0, keepdims=True)
        out = mixed_ref[:, span] * scale + matmul(values, expo.astype(BF16))
        out_ref[:, span] = (out * (1.0 / norm)).astype(BF16)


def weight_window(width, mp):
    cols = width // mp
    tiles = max(-(-cols * (m + 1) // LANES) - cols * m // LANES for m in range(mp))
    return cols, tiles


def window_start(m, width, mp):
    cols, tiles = weight_window(width, mp)
    first = jnp.minimum(m * cols // LANES, width // LANES - tiles)
    return first * LANES


def cut_copies(width, mp, distances, weight_ref, outs, sems):
    m = lax.axis_index("mp")
    place = lax.axis_index("seq")
    half = weight_ref.shape[0] // 2
    copies = []
    for i, (distance, out) in enumerate(zip(distances, outs)):
        count, window = out.shape
        row = place % 2 * half + place // 2 % 2 * (half - count)
        start = window_start(partner(m, distance, mp), width, mp)
        source = weight_ref.at[
            pl.ds(pl.multiple_of(row, 16), count), pl.ds(pl.multiple_of(start, LANES), window)
        ]
        copies.append(pltpu.make_async_copy(source, out, sems.at[i]))
    return copies


def turn_kernel(width, mp, split, sequence, *refs):
    pieces, (weight_ref, out_ref, own_ref, sem) = list(refs[:-5]), refs[-4:]
    half, window = own_ref.shape
    (copy,) = cut_copies(width, mp, [0], weight_ref, [own_ref], sem)
    copy.start()
    chip = lax.axis_index("seq") // 2 % 2
    copy.wait()
    blocks = {-1: own_ref[...]}
    for i in sequence:
        block = pieces.pop(0)[...]
        if split[i]:
            other = pieces.pop(0)[...]
            low = jnp.where(chip == 0, block, other)
            high = jnp.where(chip == 0, other, block)
            block = jnp.concatenate([low, high], axis=0)
        blocks[i] = block
    for i in range(0, mp, 2):
        pair = jnp.concatenate([blocks[i - 1], blocks[i]], axis=0)
        out_ref[:, i * half : (i + 2) * half] = pair.T


def collect_kernel(pairs, *refs):
    heads, out_ref = refs[:-1], refs[-1]
    head, rows = heads[0].shape
    half = head // 2
    core = lax.axis_index("seq") % 2
    for place in range(2):
        row = pl.multiple_of((core if place == 0 else 1 - core) * half, half)
        for i in range(pairs):
            to = (place * pairs + i) * half
            if i < len(heads):
                out_ref[to : to + half, :] = heads[i][pl.ds(row, half), :]
            else:
                out_ref[to : to + half, :] = jnp.zeros((half, rows), BF16)


def first_heads_kernel(mine_ref, theirs_ref, heads_ref, out_ref):
    half = mine_ref.shape[1]
    chunk = max(c for c in range(16, 513, 16) if mine_ref.shape[0] % c == 0)
    for start in range(0, mine_ref.shape[0], chunk):
        span = slice(start, start + chunk)
        total = matmul(mine_ref[span, :], heads_ref[:half, :])
        out_ref[span, :] = total + matmul(theirs_ref[span, :], heads_ref[half:, :])


def output_kernel(width, mp, chunk, mine_ref, theirs_ref, first_ref, last_ref, *refs):
    out_ref, heads_ref, buf_ref, sems = refs
    cols = out_ref.shape[0]
    head = last_ref.shape[0]
    half = head // 2
    m = lax.axis_index("mp")
    offset = m * cols - window_start(m, width, mp)
    core = lax.axis_index("seq") % 2
    heads_ref[...] = jnp.zeros_like(heads_ref)
    for place in range(2):
        row = pl.multiple_of((core if place == 0 else 1 - core) * half, half)
        heads_ref[place * head + half : (place + 1) * head, :] = last_ref[pl.ds(row, half), :]
    copies = []
    for i in range(cols // chunk):
        span = pl.ds(i * chunk, chunk)
        rows = pl.ds(pl.multiple_of(offset + i * chunk, 16), chunk)
        weight = jnp.concatenate([mine_ref[rows, -LANES:], theirs_ref[rows, -LANES:]], axis=1)
        total = first_ref[rows, :] + matmul(weight, heads_ref[...])
        buf_ref[span, :] = total.astype(BF16)
        copies.append(pltpu.make_async_copy(buf_ref.at[span, :], out_ref.at[span, :], sems.at[i]))
        copies[-1].start()
    for copy in copies:
        copy.wait()


def per_device(hidden_in, norm_gain, query_weight, kv_weight, out_weight):
    rows, width = hidden_in.shape
    head = query_weight.shape[1]
    mp = lax.axis_size("mp")
    assert 2 * rows == WINDOW and width == sum(BLOCKS) and head == LANES
    cols, tiles = weight_window(width, mp)
    window = tiles * LANES
    half = head // 2
    gain = norm_gain.reshape(width // LANES, LANES)
    anywhere = pl.BlockSpec(memory_space=pl.ANY)
    hbm = pl.BlockSpec(memory_space=pltpu.HBM)
    vmem = pl.BlockSpec(memory_space=pltpu.VMEM)
    dma = pltpu.SemaphoreType.DMA
    shape = lambda *dims: jax.ShapeDtypeStruct(dims, BF16)
    large = 52 * 2**20

    order = [3, 1, 2] if mp == 4 else list(range(1, mp))
    split = [mp == 4 and d == 3 for d in order]
    counts = [half // 2 if in_two else half for in_two in split]
    scale = math.log2(math.e) / math.sqrt(168.0)
    queries, kv, *pieces = call(
        functools.partial(project_all_kernel, scale, width, mp, BLOCKS, AHEAD, order),
        "project",
        [shape(rows, head), shape(2 * rows, head)] + [shape(c, window) for c in counts],
        vmem=large,
        in_specs=[hbm, vmem, hbm, hbm, hbm],
        out_specs=[vmem] * (2 + len(order)),
        scratch_shapes=project_scratch(rows, width, 3 * head, head) + [dma((len(order),))],
    )(hidden_in, gain, kv_weight, query_weight, out_weight)
    far = around(kv, "seq", 2)
    mine = [exchanged(piece, d) for d, piece in zip(order, pieces)]
    passed = call(
        pass_kernel,
        "pass_on",
        shape(*kv.shape),
        in_specs=[vmem] * 2,
        out_specs=vmem,
    )(kv, far)
    near = other_core(passed)
    mixed, stats = call(
        mixed_kernel,
        "mixed_blocks",
        [jax.ShapeDtypeStruct((head, rows), F32), jax.ShapeDtypeStruct((2, rows), F32)],
        flops=MIXED_COST,
        in_specs=[vmem] * 3,
        out_specs=[vmem] * 2,
    )(queries, kv, far)
    head_out = call(
        near_kernel,
        "near_block",
        shape(head, rows),
        in_specs=[vmem] * 4,
        out_specs=vmem,
    )(queries, near, mixed, stats)
    heads = [head_out] + [exchanged(head_out, d) for d in order[:-1]]
    if mp == 4:
        last_head = exchanged(heads[1], 1)
    else:
        last_head = exchanged(head_out, order[-1])

    parts = []
    sequence = sorted(range(mp - 1), key=lambda i: (not split[i], -order[i]))
    for i in sequence:
        parts += [mine[i], next_chip(mine[i])] if split[i] else [mine[i]]
    mine_turned = call(
        functools.partial(turn_kernel, width, mp, split, sequence),
        "turn_weight",
        shape(window, mp * half),
        in_specs=[vmem] * len(parts) + [anywhere, hbm],
        out_specs=vmem,
        scratch_shapes=[pltpu.VMEM((half, window), BF16), dma((1,))],
    )(*parts, head_out, out_weight)
    theirs_turned = other_core(mine_turned)
    taken = call(
        functools.partial(collect_kernel, mp),
        "collect_heads",
        shape(mp * head, rows),
        flops=3 * 10**10,
        in_specs=[vmem] * (mp - 1),
        out_specs=vmem,
    )(*heads)
    first_sum = call(
        first_heads_kernel,
        "first_heads",
        jax.ShapeDtypeStruct((window, rows), F32),
        in_specs=[vmem] * 3,
        out_specs=vmem,
    )(mine_turned, theirs_turned, taken)

    chunk = max(c for c in range(16, min(cols, 224) + 1, 16) if cols % c == 0)
    return call(
        functools.partial(output_kernel, width, mp, chunk),
        "output",
        shape(cols, rows),
        in_specs=[vmem] * 4,
        out_specs=hbm,
        scratch_shapes=[
            pltpu.VMEM((2 * head, rows), BF16),
            pltpu.VMEM((cols, rows), BF16),
            dma((cols // chunk,)),
        ],
    )(mine_turned, theirs_turned, first_sum, last_head)


def solution(mesh):
    in_specs = (P("seq", None), P(), P(None, "mp"), P(None, "mp"), P("mp", None))
    out_specs = P("mp", "seq")
    return jax.shard_map(
        per_device, mesh=mesh, in_specs=in_specs, out_specs=out_specs, check_vma=False
    )
```

```python
import functools
import math

import jax
import jax.numpy as jnp
import numpy as np
from jax import lax
from jax.experimental import pallas as pl
from jax.experimental.pallas import tpu as pltpu
from jax.sharding import PartitionSpec as P

WINDOW = 1024
LANES = 128
MASKED = -1e30
F32 = jnp.float32
BF16 = jnp.bfloat16


def around(block, axis, distance):
    size = lax.axis_size(axis)
    return lax.ppermute(block, axis, [(i, (i + distance) % size) for i in range(size)])


def other_core(block):
    return lax.ppermute(block, "seq", [(i, i ^ 1) for i in range(lax.axis_size("seq"))])


def next_chip(block):
    return lax.ppermute(block, "seq", [(i, i ^ 2) for i in range(lax.axis_size("seq"))])


def partner(m, distance, mp):
    return m ^ distance if mp == 4 else (m + distance) % mp


def exchanged(block, distance):
    mp = lax.axis_size("mp")
    return lax.ppermute(block, "mp", [(i, partner(i, distance, mp)) for i in range(mp)])


def call(kernel, name, out_shape, vmem=16 * 2**20, flops=1, **kwargs):
    return pl.pallas_call(
        kernel,
        name=name,
        out_shape=out_shape,
        cost_estimate=pl.CostEstimate(flops=flops, bytes_accessed=1, transcendentals=0),
        compiler_params=pltpu.CompilerParams(vmem_limit_bytes=vmem),
        **kwargs,
    )


def matmul(left, right, dims=((1,), (0,))):
    return lax.dot_general(left, right, (dims, ((), ())), preferred_element_type=F32)


def rope_factors(rope_ref, first_pos):
    rows, head = rope_ref.shape[1:]
    half = head // 2
    step = 8

    def turn(count, stride, start):
        lane = lax.broadcasted_iota(jnp.int32, (count, head), 1)
        low = lane < half
        freq = jnp.exp(
            jnp.where(low, lane, lane - half).astype(F32) * (-math.log(10000.0) * 2.0 / head)
        )
        place = lax.broadcasted_iota(jnp.int32, (count, head), 0) * stride + start
        angle = place.astype(F32) * freq
        return jnp.cos(angle), jnp.sin(angle), jnp.where(low, -1.0, 1.0)

    fine_cos, fine_sin, _ = turn(step, 1, 0)
    coarse_cos, coarse_sin, sign = turn(rows // step, step, first_pos)
    for a in range(rows // step):
        span = slice(a * step, (a + 1) * step)
        c, s = coarse_cos[a : a + 1, :], coarse_sin[a : a + 1, :]
        rope_ref[0, span, :] = c * fine_cos - s * fine_sin
        rope_ref[1, span, :] = (s * fine_cos + c * fine_sin) * sign[:step, :]


def rope(tensor, cosine, sine):
    return tensor * cosine + pltpu.roll(tensor, tensor.shape[1] // 2, 1) * sine


def project_kernel(blocks, ahead, x_ref, gain_ref, weight_refs, *scratch):
    x_buf, weight_buf, rope_buf, scaled_ref, total_ref, square_ref, sems = scratch
    rows, width = x_ref.shape
    copies = []
    ends = [sum(blocks[: k + 1]) for k in range(len(blocks))]
    for k, (size, end) in enumerate(zip(blocks, ends)):
        part = pl.ds(end - size, size)
        group = [pltpu.make_async_copy(x_ref.at[:, part], x_buf.at[:, part], sems.at[0, k])]
        first = 0
        for i, weight_ref in enumerate(weight_refs):
            to = weight_buf.at[part, pl.ds(first, weight_ref.shape[1])]
            group.append(pltpu.make_async_copy(weight_ref.at[part, :], to, sems.at[1 + i, k]))
            first += weight_ref.shape[1]
        copies.append(group)
    for pair in copies[:ahead]:
        for copy in pair:
            copy.start()
    rope_factors(rope_buf, lax.axis_index("seq") * rows)
    chunk = 64
    for k, (size, end) in enumerate(zip(blocks, ends)):
        for copy in copies[k]:
            copy.wait()
        if k + ahead < len(blocks):
            for copy in copies[k + ahead]:
                copy.start()
        for r in range(0, rows, chunk):
            part = None
            for t in range(end - size, end, LANES):
                x = x_buf[r : r + chunk, t : t + LANES]
                gain = gain_ref[t // LANES : t // LANES + 1, :].astype(BF16)
                scaled_ref[r : r + chunk, t : t + LANES] = x * gain
                x = x.astype(F32)
                square = x * x
                part = square if part is None else part + square
            square_ref[r : r + chunk, :] = part if k == 0 else square_ref[r : r + chunk, :] + part
        span = slice(end - size, end)
        product = matmul(scaled_ref[:, span], weight_buf[span, :])
        total_ref[...] = product if k == 0 else total_ref[...] + product
    mean = jnp.sum(square_ref[...], axis=1, keepdims=True) * (1.0 / width)
    return lax.rsqrt(mean + 1e-06)


def project_all_kernel(scale, width, mp, blocks, ahead, cut, x_ref, gain_ref, *refs):
    kv_weight_ref, query_weight_ref, out_weight_ref, *refs = refs
    queries_ref, kv_ref, *refs = refs
    pieces, scratch, cut_sems = refs[: len(cut)], refs[len(cut) : -1], refs[-1]
    copies = cut_copies(width, mp, cut, out_weight_ref, pieces, cut_sems)
    for copy in copies:
        copy.start()
    weights = (kv_weight_ref, query_weight_ref)
    inverse = project_kernel(blocks, ahead, x_ref, gain_ref, weights, *scratch)
    rope_buf, total_ref = scratch[2], scratch[4]
    rows, head = queries_ref.shape
    cosine, sine = rope_buf[0], rope_buf[1]
    kv_ref[:rows, :] = rope(total_ref[:, :head] * inverse, cosine, sine).astype(BF16)
    for t in range(rows // LANES):
        span = slice(t * LANES, (t + 1) * LANES)
        values = total_ref[span, head : 2 * head] * inverse[span, :]
        kv_ref[rows + t * head : rows + (t + 1) * head, :] = values.T.astype(BF16)
    queries = rope(total_ref[:, 2 * head :] * (inverse * scale), cosine, sine)
    queries_ref[...] = queries.astype(BF16)
    for copy in copies:
        copy.wait()


BLOCKS = (768,) * 7
AHEAD = 5
MIXED_COST = 10**11


def project_scratch(rows, width, cols, head):
    return [
        pltpu.VMEM((rows, width), BF16),
        pltpu.VMEM((width, cols), BF16),
        pltpu.VMEM((2, rows, head), F32),
        pltpu.VMEM((rows, width), BF16),
        pltpu.VMEM((rows, cols), F32),
        pltpu.VMEM((rows, LANES), F32),
        pltpu.SemaphoreType.DMA((3, len(BLOCKS))),
    ]


def values_of(block_ref, start):
    head = block_ref.shape[1]
    tiles = [block_ref[r : r + head, :] for r in range(start, block_ref.shape[0], head)]
    return jnp.concatenate(tiles, axis=1)


def pass_kernel(own_ref, far_ref, out_ref):
    core = lax.axis_index("seq") % 2
    out_ref[...] = jnp.where(core == 0, own_ref[...], far_ref[...])


NT = ((1,), (1,))


def mixed_kernel(q_ref, own_ref, far_ref, out_ref, stats_ref):
    rows = q_ref.shape[0]
    chunk = rows
    bias = jnp.where(lax.axis_index("seq") < 2, MASKED, 0.0).astype(F32)
    own_values, far_values = values_of(own_ref, rows), values_of(far_ref, rows)
    for start in range(0, rows, chunk):
        span = slice(start, start + chunk)
        q = q_ref[span, :]
        key_index = lax.broadcasted_iota(jnp.int32, (rows, chunk), 0)
        query_index = lax.broadcasted_iota(jnp.int32, (rows, chunk), 1) + start
        own = key_index <= query_index
        far = matmul(far_ref[:rows, :], q, NT) + bias
        scores = jnp.where(own, matmul(own_ref[:rows, :], q, NT), far)
        highest = jnp.max(scores, axis=0, keepdims=True)
        expo = jnp.exp2(scores - highest)
        stats_ref[0:1, span] = highest
        stats_ref[1:2, span] = jnp.sum(expo, axis=0, keepdims=True)
        out = matmul(own_values, jnp.where(own, expo, 0.0).astype(BF16))
        out_ref[:, span] = out + matmul(far_values, jnp.where(own, 0.0, expo).astype(BF16))


def near_kernel(q_ref, near_ref, mixed_ref, stats_ref, out_ref):
    rows = q_ref.shape[0]
    chunk = rows
    bias = jnp.where(lax.axis_index("seq") < 1, MASKED, 0.0).astype(F32)
    values = values_of(near_ref, rows)
    for start in range(0, rows, chunk):
        span = slice(start, start + chunk)
        scores = matmul(near_ref[:rows, :], q_ref[span, :], NT) + bias
        before = stats_ref[0:1, span]
        highest = jnp.maximum(before, jnp.max(scores, axis=0, keepdims=True))
        expo = jnp.exp2(scores - highest)
        scale = jnp.exp2(before - highest)
        norm = stats_ref[1:2, span] * scale + jnp.sum(expo, axis=0, keepdims=True)
        out = mixed_ref[:, span] * scale + matmul(values, expo.astype(BF16))
        out_ref[:, span] = (out * (1.0 / norm)).astype(BF16)


def weight_window(width, mp):
    cols = width // mp
    tiles = max(-(-cols * (m + 1) // LANES) - cols * m // LANES for m in range(mp))
    return cols, tiles


def window_start(m, width, mp):
    cols, tiles = weight_window(width, mp)
    first = jnp.minimum(m * cols // LANES, width // LANES - tiles)
    return first * LANES


def cut_copies(width, mp, distances, weight_ref, outs, sems):
    m = lax.axis_index("mp")
    place = lax.axis_index("seq")
    half = weight_ref.shape[0] // 2
    copies = []
    for i, (distance, out) in enumerate(zip(distances, outs)):
        count, window = out.shape
        row = place % 2 * half + place // 2 % 2 * (half - count)
        start = window_start(partner(m, distance, mp), width, mp)
        source = weight_ref.at[
            pl.ds(pl.multiple_of(row, 16), count), pl.ds(pl.multiple_of(start, LANES), window)
        ]
        copies.append(pltpu.make_async_copy(source, out, sems.at[i]))
    return copies


def turn_kernel(width, mp, split, sequence, *refs):
    pieces, (weight_ref, out_ref, own_ref, sem) = list(refs[:-5]), refs[-4:]
    half, window = own_ref.shape
    (copy,) = cut_copies(width, mp, [0], weight_ref, [own_ref], sem)
    copy.start()
    chip = lax.axis_index("seq") // 2 % 2
    copy.wait()
    blocks = {-1: own_ref[...]}
    for i in sequence:
        block = pieces.pop(0)[...]
        if split[i]:
            other = pieces.pop(0)[...]
            low = jnp.where(chip == 0, block, other)
            high = jnp.where(chip == 0, other, block)
            block = jnp.concatenate([low, high], axis=0)
        blocks[i] = block
    for i in range(0, mp, 2):
        pair = jnp.concatenate([blocks[i - 1], blocks[i]], axis=0)
        out_ref[:, i * half : (i + 2) * half] = pair.T


def collect_kernel(pairs, *refs):
    heads, out_ref = refs[:-1], refs[-1]
    head, rows = heads[0].shape
    half = head // 2
    core = lax.axis_index("seq") % 2
    for place in range(2):
        row = pl.multiple_of((core if place == 0 else 1 - core) * half, half)
        for i in range(pairs):
            to = (place * pairs + i) * half
            if i < len(heads):
                out_ref[to : to + half, :] = heads[i][pl.ds(row, half), :]
            else:
                out_ref[to : to + half, :] = jnp.zeros((half, rows), BF16)


def first_heads_kernel(mine_ref, theirs_ref, heads_ref, out_ref):
    half = mine_ref.shape[1]
    chunk = max(c for c in range(16, 513, 16) if mine_ref.shape[0] % c == 0)
    for start in range(0, mine_ref.shape[0], chunk):
        span = slice(start, start + chunk)
        total = matmul(mine_ref[span, :], heads_ref[:half, :])
        out_ref[span, :] = total + matmul(theirs_ref[span, :], heads_ref[half:, :])


def output_kernel(width, mp, chunk, mine_ref, theirs_ref, first_ref, last_ref, *refs):
    out_ref, heads_ref, buf_ref, sems = refs
    cols = out_ref.shape[0]
    head = last_ref.shape[0]
    half = head // 2
    m = lax.axis_index("mp")
    offset = m * cols - window_start(m, width, mp)
    core = lax.axis_index("seq") % 2
    heads_ref[...] = jnp.zeros_like(heads_ref)
    for place in range(2):
        row = pl.multiple_of((core if place == 0 else 1 - core) * half, half)
        heads_ref[place * head + half : (place + 1) * head, :] = last_ref[pl.ds(row, half), :]
    copies = []
    for i in range(cols // chunk):
        span = pl.ds(i * chunk, chunk)
        rows = pl.ds(pl.multiple_of(offset + i * chunk, 16), chunk)
        weight = jnp.concatenate([mine_ref[rows, -LANES:], theirs_ref[rows, -LANES:]], axis=1)
        total = first_ref[rows, :] + matmul(weight, heads_ref[...])
        buf_ref[span, :] = total.astype(BF16)
        copies.append(pltpu.make_async_copy(buf_ref.at[span, :], out_ref.at[span, :], sems.at[i]))
        copies[-1].start()
    for copy in copies:
        copy.wait()


def per_device(hidden_in, norm_gain, query_weight, kv_weight, out_weight):
    rows, width = hidden_in.shape
    head = query_weight.shape[1]
    mp = lax.axis_size("mp")
    assert 2 * rows == WINDOW and width == sum(BLOCKS) and head == LANES
    cols, tiles = weight_window(width, mp)
    window = tiles * LANES
    half = head // 2
    gain = norm_gain.reshape(width // LANES, LANES)
    anywhere = pl.BlockSpec(memory_space=pl.ANY)
    hbm = pl.BlockSpec(memory_space=pltpu.HBM)
    vmem = pl.BlockSpec(memory_space=pltpu.VMEM)
    dma = pltpu.SemaphoreType.DMA
    shape = lambda *dims: jax.ShapeDtypeStruct(dims, BF16)
    large = 52 * 2**20

    order = [3, 1, 2] if mp == 4 else list(range(1, mp))
    split = [mp == 4 and d == 3 for d in order]
    counts = [half // 2 if in_two else half for in_two in split]
    scale = math.log2(math.e) / math.sqrt(168.0)
    queries, kv, *pieces = call(
        functools.partial(project_all_kernel, scale, width, mp, BLOCKS, AHEAD, order),
        "project",
        [shape(rows, head), shape(2 * rows, head)] + [shape(c, window) for c in counts],
        vmem=large,
        in_specs=[hbm, vmem, hbm, hbm, hbm],
        out_specs=[vmem] * (2 + len(order)),
        scratch_shapes=project_scratch(rows, width, 3 * head, head) + [dma((len(order),))],
    )(hidden_in, gain, kv_weight, query_weight, out_weight)
    far = around(kv, "seq", 2)
    mine = [exchanged(piece, d) for d, piece in zip(order, pieces)]
    passed = call(
        pass_kernel,
        "pass_on",
        shape(*kv.shape),
        in_specs=[vmem] * 2,
        out_specs=vmem,
    )(kv, far)
    near = other_core(passed)
    mixed, stats = call(
        mixed_kernel,
        "mixed_blocks",
        [jax.ShapeDtypeStruct((head, rows), F32), jax.ShapeDtypeStruct((2, rows), F32)],
        flops=MIXED_COST,
        in_specs=[vmem] * 3,
        out_specs=[vmem] * 2,
    )(queries, kv, far)
    head_out = call(
        near_kernel,
        "near_block",
        shape(head, rows),
        in_specs=[vmem] * 4,
        out_specs=vmem,
    )(queries, near, mixed, stats)
    heads = [head_out] + [exchanged(head_out, d) for d in order[:-1]]
    if mp == 4:
        last_head = exchanged(heads[1], 1)
    else:
        last_head = exchanged(head_out, order[-1])

    parts = []
    sequence = sorted(range(mp - 1), key=lambda i: (not split[i], -order[i]))
    for i in sequence:
        parts += [mine[i], next_chip(mine[i])] if split[i] else [mine[i]]
    mine_turned = call(
        functools.partial(turn_kernel, width, mp, split, sequence),
        "turn_weight",
        shape(window, mp * half),
        in_specs=[vmem] * len(parts) + [anywhere, hbm],
        out_specs=vmem,
        scratch_shapes=[pltpu.VMEM((half, window), BF16), dma((1,))],
    )(*parts, head_out, out_weight)
    theirs_turned = other_core(mine_turned)
    taken = call(
        functools.partial(collect_kernel, mp),
        "collect_heads",
        shape(mp * head, rows),
        flops=3 * 10**10,
        in_specs=[vmem] * (mp - 1),
        out_specs=vmem,
    )(*heads)
    first_sum = call(
        first_heads_kernel,
        "first_heads",
        jax.ShapeDtypeStruct((window, rows), F32),
        in_specs=[vmem] * 3,
        out_specs=vmem,
    )(mine_turned, theirs_turned, taken)

    chunk = max(c for c in range(16, min(cols, 224) + 1, 16) if cols % c == 0)
    return call(
        functools.partial(output_kernel, width, mp, chunk),
        "output",
        shape(cols, rows),
        in_specs=[vmem] * 4,
        out_specs=hbm,
        scratch_shapes=[
            pltpu.VMEM((2 * head, rows), BF16),
            pltpu.VMEM((cols, rows), BF16),
            dma((cols // chunk,)),
        ],
    )(mine_turned, theirs_turned, first_sum, last_head)


def solution(mesh):
    in_specs = (P("seq", None), P(), P(None, "mp"), P(None, "mp"), P("mp", None))
    out_specs = P("mp", "seq")
    return jax.shard_map(
        per_device, mesh=mesh, in_specs=in_specs, out_specs=out_specs, check_vma=False
    )
```

```python
import functools
import math

import jax
import jax.numpy as jnp
import numpy as np
from jax import lax
from jax.experimental import pallas as pl
from jax.experimental.pallas import tpu as pltpu
from jax.sharding import PartitionSpec as P

WINDOW = 1024
LANES = 128
MASKED = -1e30
F32 = jnp.float32
BF16 = jnp.bfloat16


def around(block, axis, distance):
    size = lax.axis_size(axis)
    return lax.ppermute(block, axis, [(i, (i + distance) % size) for i in range(size)])


def other_core(block):
    return lax.ppermute(block, "seq", [(i, i ^ 1) for i in range(lax.axis_size("seq"))])


def next_chip(block):
    return lax.ppermute(block, "seq", [(i, i ^ 2) for i in range(lax.axis_size("seq"))])


def partner(m, distance, mp):
    return m ^ distance if mp == 4 else (m + distance) % mp


def exchanged(block, distance):
    mp = lax.axis_size("mp")
    return lax.ppermute(block, "mp", [(i, partner(i, distance, mp)) for i in range(mp)])


def call(kernel, name, out_shape, vmem=16 * 2**20, flops=1, **kwargs):
    return pl.pallas_call(
        kernel,
        name=name,
        out_shape=out_shape,
        cost_estimate=pl.CostEstimate(flops=flops, bytes_accessed=1, transcendentals=0),
        compiler_params=pltpu.CompilerParams(vmem_limit_bytes=vmem),
        **kwargs,
    )


def matmul(left, right, dims=((1,), (0,))):
    return lax.dot_general(left, right, (dims, ((), ())), preferred_element_type=F32)


def rope_factors(rope_ref, first_pos):
    rows, head = rope_ref.shape[1:]
    half = head // 2
    step = 8

    def turn(count, stride, start):
        lane = lax.broadcasted_iota(jnp.int32, (count, head), 1)
        low = lane < half
        freq = jnp.exp(
            jnp.where(low, lane, lane - half).astype(F32) * (-math.log(10000.0) * 2.0 / head)
        )
        place = lax.broadcasted_iota(jnp.int32, (count, head), 0) * stride + start
        angle = place.astype(F32) * freq
        return jnp.cos(angle), jnp.sin(angle), jnp.where(low, -1.0, 1.0)

    fine_cos, fine_sin, _ = turn(step, 1, 0)
    coarse_cos, coarse_sin, sign = turn(rows // step, step, first_pos)
    for a in range(rows // step):
        span = slice(a * step, (a + 1) * step)
        c, s = coarse_cos[a : a + 1, :], coarse_sin[a : a + 1, :]
        rope_ref[0, span, :] = c * fine_cos - s * fine_sin
        rope_ref[1, span, :] = (s * fine_cos + c * fine_sin) * sign[:step, :]


def rope(tensor, cosine, sine):
    return tensor * cosine + pltpu.roll(tensor, tensor.shape[1] // 2, 1) * sine


def project_kernel(blocks, ahead, x_ref, gain_ref, weight_refs, *scratch):
    x_buf, weight_buf, rope_buf, scaled_ref, total_ref, square_ref, sems = scratch
    rows, width = x_ref.shape
    copies = []
    ends = [sum(blocks[: k + 1]) for k in range(len(blocks))]
    for k, (size, end) in enumerate(zip(blocks, ends)):
        part = pl.ds(end - size, size)
        group = [pltpu.make_async_copy(x_ref.at[:, part], x_buf.at[:, part], sems.at[0, k])]
        first = 0
        for i, weight_ref in enumerate(weight_refs):
            to = weight_buf.at[part, pl.ds(first, weight_ref.shape[1])]
            group.append(pltpu.make_async_copy(weight_ref.at[part, :], to, sems.at[1 + i, k]))
            first += weight_ref.shape[1]
        copies.append(group)
    for pair in copies[:ahead]:
        for copy in pair:
            copy.start()
    rope_factors(rope_buf, lax.axis_index("seq") * rows)
    chunk = 64
    for k, (size, end) in enumerate(zip(blocks, ends)):
        for copy in copies[k]:
            copy.wait()
        if k + ahead < len(blocks):
            for copy in copies[k + ahead]:
                copy.start()
        for r in range(0, rows, chunk):
            part = None
            for t in range(end - size, end, LANES):
                x = x_buf[r : r + chunk, t : t + LANES]
                gain = gain_ref[t // LANES : t // LANES + 1, :].astype(BF16)
                scaled_ref[r : r + chunk, t : t + LANES] = x * gain
                x = x.astype(F32)
                square = x * x
                part = square if part is None else part + square
            square_ref[r : r + chunk, :] = part if k == 0 else square_ref[r : r + chunk, :] + part
        span = slice(end - size, end)
        product = matmul(scaled_ref[:, span], weight_buf[span, :])
        total_ref[...] = product if k == 0 else total_ref[...] + product
    mean = jnp.sum(square_ref[...], axis=1, keepdims=True) * (1.0 / width)
    return lax.rsqrt(mean + 1e-06)


def project_all_kernel(scale, width, mp, blocks, ahead, cut, x_ref, gain_ref, *refs):
    kv_weight_ref, query_weight_ref, out_weight_ref, *refs = refs
    queries_ref, kv_ref, *refs = refs
    pieces, scratch, cut_sems = refs[: len(cut)], refs[len(cut) : -1], refs[-1]
    copies = cut_copies(width, mp, cut, out_weight_ref, pieces, cut_sems)
    for copy in copies:
        copy.start()
    weights = (kv_weight_ref, query_weight_ref)
    inverse = project_kernel(blocks, ahead, x_ref, gain_ref, weights, *scratch)
    rope_buf, total_ref = scratch[2], scratch[4]
    rows, head = queries_ref.shape
    cosine, sine = rope_buf[0], rope_buf[1]
    kv_ref[:rows, :] = rope(total_ref[:, :head] * inverse, cosine, sine).astype(BF16)
    for t in range(rows // LANES):
        span = slice(t * LANES, (t + 1) * LANES)
        values = total_ref[span, head : 2 * head] * inverse[span, :]
        kv_ref[rows + t * head : rows + (t + 1) * head, :] = values.T.astype(BF16)
    queries = rope(total_ref[:, 2 * head :] * (inverse * scale), cosine, sine)
    queries_ref[...] = queries.astype(BF16)
    for copy in copies:
        copy.wait()


BLOCKS = (768,) * 7
AHEAD = 7
MIXED_COST = 10**11


def project_scratch(rows, width, cols, head):
    return [
        pltpu.VMEM((rows, width), BF16),
        pltpu.VMEM((width, cols), BF16),
        pltpu.VMEM((2, rows, head), F32),
        pltpu.VMEM((rows, width), BF16),
        pltpu.VMEM((rows, cols), F32),
        pltpu.VMEM((rows, LANES), F32),
        pltpu.SemaphoreType.DMA((3, len(BLOCKS))),
    ]


def values_of(block_ref, start):
    head = block_ref.shape[1]
    tiles = [block_ref[r : r + head, :] for r in range(start, block_ref.shape[0], head)]
    return jnp.concatenate(tiles, axis=1)


def pass_kernel(own_ref, far_ref, out_ref):
    core = lax.axis_index("seq") % 2
    out_ref[...] = jnp.where(core == 0, own_ref[...], far_ref[...])


NT = ((1,), (1,))


def mixed_kernel(q_ref, own_ref, far_ref, out_ref, stats_ref):
    rows = q_ref.shape[0]
    chunk = rows
    bias = jnp.where(lax.axis_index("seq") < 2, MASKED, 0.0).astype(F32)
    own_values, far_values = values_of(own_ref, rows), values_of(far_ref, rows)
    for start in range(0, rows, chunk):
        span = slice(start, start + chunk)
        q = q_ref[span, :]
        key_index = lax.broadcasted_iota(jnp.int32, (rows, chunk), 0)
        query_index = lax.broadcasted_iota(jnp.int32, (rows, chunk), 1) + start
        own = key_index <= query_index
        far = matmul(far_ref[:rows, :], q, NT) + bias
        scores = jnp.where(own, matmul(own_ref[:rows, :], q, NT), far)
        highest = jnp.max(scores, axis=0, keepdims=True)
        expo = jnp.exp2(scores - highest)
        stats_ref[0:1, span] = highest
        stats_ref[1:2, span] = jnp.sum(expo, axis=0, keepdims=True)
        out = matmul(own_values, jnp.where(own, expo, 0.0).astype(BF16))
        out_ref[:, span] = out + matmul(far_values, jnp.where(own, 0.0, expo).astype(BF16))


def near_kernel(q_ref, near_ref, mixed_ref, stats_ref, out_ref):
    rows = q_ref.shape[0]
    chunk = rows
    bias = jnp.where(lax.axis_index("seq") < 1, MASKED, 0.0).astype(F32)
    values = values_of(near_ref, rows)
    for start in range(0, rows, chunk):
        span = slice(start, start + chunk)
        scores = matmul(near_ref[:rows, :], q_ref[span, :], NT) + bias
        before = stats_ref[0:1, span]
        highest = jnp.maximum(before, jnp.max(scores, axis=0, keepdims=True))
        expo = jnp.exp2(scores - highest)
        scale = jnp.exp2(before - highest)
        norm = stats_ref[1:2, span] * scale + jnp.sum(expo, axis=0, keepdims=True)
        out = mixed_ref[:, span] * scale + matmul(values, expo.astype(BF16))
        out_ref[:, span] = (out * (1.0 / norm)).astype(BF16)


def weight_window(width, mp):
    cols = width // mp
    tiles = max(-(-cols * (m + 1) // LANES) - cols * m // LANES for m in range(mp))
    return cols, tiles


def window_start(m, width, mp):
    cols, tiles = weight_window(width, mp)
    first = jnp.minimum(m * cols // LANES, width // LANES - tiles)
    return first * LANES


def cut_copies(width, mp, distances, weight_ref, outs, sems):
    m = lax.axis_index("mp")
    place = lax.axis_index("seq")
    half = weight_ref.shape[0] // 2
    copies = []
    for i, (distance, out) in enumerate(zip(distances, outs)):
        count, window = out.shape
        row = place % 2 * half + place // 2 % 2 * (half - count)
        start = window_start(partner(m, distance, mp), width, mp)
        source = weight_ref.at[
            pl.ds(pl.multiple_of(row, 16), count), pl.ds(pl.multiple_of(start, LANES), window)
        ]
        copies.append(pltpu.make_async_copy(source, out, sems.at[i]))
    return copies


def turn_kernel(width, mp, split, sequence, *refs):
    pieces, (weight_ref, out_ref, own_ref, sem) = list(refs[:-5]), refs[-4:]
    half, window = own_ref.shape
    (copy,) = cut_copies(width, mp, [0], weight_ref, [own_ref], sem)
    copy.start()
    chip = lax.axis_index("seq") // 2 % 2
    copy.wait()
    blocks = {-1: own_ref[...]}
    for i in sequence:
        block = pieces.pop(0)[...]
        if split[i]:
            other = pieces.pop(0)[...]
            low = jnp.where(chip == 0, block, other)
            high = jnp.where(chip == 0, other, block)
            block = jnp.concatenate([low, high], axis=0)
        blocks[i] = block
    for i in range(0, mp, 2):
        pair = jnp.concatenate([blocks[i - 1], blocks[i]], axis=0)
        out_ref[:, i * half : (i + 2) * half] = pair.T


def collect_kernel(pairs, *refs):
    heads, out_ref = refs[:-1], refs[-1]
    head, rows = heads[0].shape
    half = head // 2
    core = lax.axis_index("seq") % 2
    for place in range(2):
        row = pl.multiple_of((core if place == 0 else 1 - core) * half, half)
        for i in range(pairs):
            to = (place * pairs + i) * half
            if i < len(heads):
                out_ref[to : to + half, :] = heads[i][pl.ds(row, half), :]
            else:
                out_ref[to : to + half, :] = jnp.zeros((half, rows), BF16)


def first_heads_kernel(mine_ref, theirs_ref, heads_ref, out_ref):
    half = mine_ref.shape[1]
    chunk = max(c for c in range(16, 513, 16) if mine_ref.shape[0] % c == 0)
    for start in range(0, mine_ref.shape[0], chunk):
        span = slice(start, start + chunk)
        total = matmul(mine_ref[span, :], heads_ref[:half, :])
        out_ref[span, :] = total + matmul(theirs_ref[span, :], heads_ref[half:, :])


def output_kernel(width, mp, chunk, mine_ref, theirs_ref, first_ref, last_ref, *refs):
    out_ref, heads_ref, buf_ref, sems = refs
    cols = out_ref.shape[0]
    head = last_ref.shape[0]
    half = head // 2
    m = lax.axis_index("mp")
    offset = m * cols - window_start(m, width, mp)
    core = lax.axis_index("seq") % 2
    heads_ref[...] = jnp.zeros_like(heads_ref)
    for place in range(2):
        row = pl.multiple_of((core if place == 0 else 1 - core) * half, half)
        heads_ref[place * head + half : (place + 1) * head, :] = last_ref[pl.ds(row, half), :]
    copies = []
    for i in range(cols // chunk):
        span = pl.ds(i * chunk, chunk)
        rows = pl.ds(pl.multiple_of(offset + i * chunk, 16), chunk)
        weight = jnp.concatenate([mine_ref[rows, -LANES:], theirs_ref[rows, -LANES:]], axis=1)
        total = first_ref[rows, :] + matmul(weight, heads_ref[...])
        buf_ref[span, :] = total.astype(BF16)
        copies.append(pltpu.make_async_copy(buf_ref.at[span, :], out_ref.at[span, :], sems.at[i]))
        copies[-1].start()
    for copy in copies:
        copy.wait()


def per_device(hidden_in, norm_gain, query_weight, kv_weight, out_weight):
    rows, width = hidden_in.shape
    head = query_weight.shape[1]
    mp = lax.axis_size("mp")
    assert 2 * rows == WINDOW and width == sum(BLOCKS) and head == LANES
    cols, tiles = weight_window(width, mp)
    window = tiles * LANES
    half = head // 2
    gain = norm_gain.reshape(width // LANES, LANES)
    anywhere = pl.BlockSpec(memory_space=pl.ANY)
    hbm = pl.BlockSpec(memory_space=pltpu.HBM)
    vmem = pl.BlockSpec(memory_space=pltpu.VMEM)
    dma = pltpu.SemaphoreType.DMA
    shape = lambda *dims: jax.ShapeDtypeStruct(dims, BF16)
    large = 52 * 2**20

    order = [3, 1, 2] if mp == 4 else list(range(1, mp))
    split = [mp == 4 and d == 3 for d in order]
    counts = [half // 2 if in_two else half for in_two in split]
    scale = math.log2(math.e) / math.sqrt(168.0)
    queries, kv, *pieces = call(
        functools.partial(project_all_kernel, scale, width, mp, BLOCKS, AHEAD, order),
        "project",
        [shape(rows, head), shape(2 * rows, head)] + [shape(c, window) for c in counts],
        vmem=large,
        in_specs=[hbm, vmem, hbm, hbm, hbm],
        out_specs=[vmem] * (2 + len(order)),
        scratch_shapes=project_scratch(rows, width, 3 * head, head) + [dma((len(order),))],
    )(hidden_in, gain, kv_weight, query_weight, out_weight)
    far = around(kv, "seq", 2)
    mine = [exchanged(piece, d) for d, piece in zip(order, pieces)]
    passed = call(
        pass_kernel,
        "pass_on",
        shape(*kv.shape),
        in_specs=[vmem] * 2,
        out_specs=vmem,
    )(kv, far)
    near = other_core(passed)
    mixed, stats = call(
        mixed_kernel,
        "mixed_blocks",
        [jax.ShapeDtypeStruct((head, rows), F32), jax.ShapeDtypeStruct((2, rows), F32)],
        flops=MIXED_COST,
        in_specs=[vmem] * 3,
        out_specs=[vmem] * 2,
    )(queries, kv, far)
    head_out = call(
        near_kernel,
        "near_block",
        shape(head, rows),
        in_specs=[vmem] * 4,
        out_specs=vmem,
    )(queries, near, mixed, stats)
    heads = [head_out] + [exchanged(head_out, d) for d in order[:-1]]
    if mp == 4:
        last_head = exchanged(heads[1], 1)
    else:
        last_head = exchanged(head_out, order[-1])

    parts = []
    sequence = sorted(range(mp - 1), key=lambda i: (not split[i], -order[i]))
    for i in sequence:
        parts += [mine[i], next_chip(mine[i])] if split[i] else [mine[i]]
    mine_turned = call(
        functools.partial(turn_kernel, width, mp, split, sequence),
        "turn_weight",
        shape(window, mp * half),
        in_specs=[vmem] * len(parts) + [anywhere, hbm],
        out_specs=vmem,
        scratch_shapes=[pltpu.VMEM((half, window), BF16), dma((1,))],
    )(*parts, head_out, out_weight)
    theirs_turned = other_core(mine_turned)
    taken = call(
        functools.partial(collect_kernel, mp),
        "collect_heads",
        shape(mp * head, rows),
        flops=3 * 10**10,
        in_specs=[vmem] * (mp - 1),
        out_specs=vmem,
    )(*heads)
    first_sum = call(
        first_heads_kernel,
        "first_heads",
        jax.ShapeDtypeStruct((window, rows), F32),
        in_specs=[vmem] * 3,
        out_specs=vmem,
    )(mine_turned, theirs_turned, taken)

    chunk = max(c for c in range(16, min(cols, 224) + 1, 16) if cols % c == 0)
    return call(
        functools.partial(output_kernel, width, mp, chunk),
        "output",
        shape(cols, rows),
        in_specs=[vmem] * 4,
        out_specs=hbm,
        scratch_shapes=[
            pltpu.VMEM((2 * head, rows), BF16),
            pltpu.VMEM((cols, rows), BF16),
            dma((cols // chunk,)),
        ],
    )(mine_turned, theirs_turned, first_sum, last_head)


def solution(mesh):
    in_specs = (P("seq", None), P(), P(None, "mp"), P(None, "mp"), P("mp", None))
    out_specs = P("mp", "seq")
    return jax.shard_map(
        per_device, mesh=mesh, in_specs=in_specs, out_specs=out_specs, check_vma=False
    )
```
